512 devices in a mesh: grp: 64 (over y, x, core), sub: 8 (over z).
Axes of the slice: x: 4, y: 8, z: 8, core: 2. Of those that a mesh axis runs over, the one named last changes fastest.
Arguments:
- velocity: float32 [3, 8192, 4096], P(None, ('grp', 'sub')), may hold values from -6 to 6
- forcing: float32 [3, 8192, 4096], P(None, ('grp', 'sub')), may hold values from -6 to 6
- viscosity: float32 [8192, 4096], P(('grp', 'sub')), may hold values from 0.2 to 2
- coarse_visc: float32 [4096, 1024], P(('grp', 'sub')), may hold values from 0.5 to 5
Outputs:
- corrected: float32 [3, 8192, 4096], P(None, ('grp', 'sub'))
- coarse_fix: float32 [3, 4096, 1024], P(None, ('grp', 'sub'))
The draws below stay inside these ranges and needn't reach their ends.
All inputs are finite; a program needn't handle non-finite values.
Results may differ from the reference program's by a relative error of at most 0.00002.
Values sent between devices are 32-bit elements; how exact they have to be, the bound alone decides.
No kernel may reach another device: no remote copies, remote signals or barrier semaphores. Data moves between devices by JAX's collectives and lax.ppermute only.
A program may use at most 128 MiB of HBM per device.

```python
import math
import jax
import jax.numpy as jnp

NY = 32
NZ = 32
DEGREE = 3
NX1 = 4096
NX2 = 8192


def steps_of(rng, shape, pieces, least, largest):
    def one(axis_at, parts):
        steps = jax.random.uniform(jax.random.fold_in(jax.random.fold_in(rng, 6), axis_at), (parts,), jnp.float32, least / len(pieces), largest / len(pieces))
        return jnp.repeat(jnp.exp(steps), shape[axis_at] // parts).reshape((-1,) + (1,) * (len(shape) - axis_at - 1))

    factor_of = one(*pieces[0])
    for cut in pieces[1:]:
        factor_of = factor_of * one(*cut)
    return factor_of


def centred(rng, dims, width, bound, cuts=(), held_as=jnp.bfloat16):
    values = jax.random.normal(rng, dims, jnp.float32) * width
    if len(cuts) > 0:
        values = steps_of(rng, dims, cuts, -0.22, 0.18) * values
    return jnp.clip(values, min=-bound, max=bound).astype(held_as)


def setup_inputs(seed: int = 0) -> dict:
    keys = jax.random.split(jax.random.key(seed), 5)
    velocity = centred(keys[0], (3, NX2, 4 * NY * NZ), 1.0, 6.0, ((1, 512),), jnp.float32)
    forcing = centred(keys[1], (3, NX2, 4 * NY * NZ), 1.0, 6.0, ((1, 512),), jnp.float32)
    viscosity = jnp.clip(jnp.exp(math.log(2.0) - 2.3025851 * jax.random.uniform(keys[2], (NX2, 4 * NY * NZ), jnp.float32) ** steps_of(keys[2], (NX2, 4 * NY * NZ), ((0, 512),), -0.2, 0.2)), 0.2, 2.0)
    coarse_visc = jnp.clip(jnp.exp(math.log(5.0) - 2.3025851 * jax.random.uniform(keys[3], (NX1, NY * NZ), jnp.float32) ** steps_of(keys[3], (NX1, NY * NZ), ((0, 512),), -0.2, 0.2)), 0.5, 5.0)
    return dict(velocity=velocity, forcing=forcing, viscosity=viscosity, coarse_visc=coarse_visc)


LOWER_EIG = 0.15
UPPER_EIG = 1.95
CENTER = 0.5 * (UPPER_EIG + LOWER_EIG)
HALF_WIDTH = 0.5 * (UPPER_EIG - LOWER_EIG)


def apply_visc(padded, coeff, rows, cols):
    planes = padded.shape[1] - 2
    blocks = padded.reshape(3, planes + 2, rows, cols)
    center = blocks[:, 1:-1]
    beside = blocks[:, 2:] + blocks[:, :-2]
    beside = beside + jnp.roll(center, 1, 2) + jnp.roll(center, -1, 2)
    beside = beside + jnp.roll(center, 1, 3) + jnp.roll(center, -1, 3)
    scaled = coeff.reshape(1, planes, rows, cols)
    return ((1.0 + 6.0 * scaled) * center - scaled * beside).reshape(3, planes, rows * cols)


def restrict_cross(field, rows, cols):
    planes = field.shape[1]
    blocks = field.reshape(3, planes, rows, cols)
    odd_rows = blocks[:, :, 1::2]
    blocks = blocks[:, :, 0::2] + 0.5 * (odd_rows + jnp.roll(odd_rows, 1, 2))
    odd_cols = blocks[:, :, :, 1::2]
    blocks = blocks[:, :, :, 0::2] + 0.5 * (odd_cols + jnp.roll(odd_cols, 1, 3))
    return blocks.reshape(3, planes, (rows // 2) * (cols // 2))


def restrict_planes(field, before):
    even_planes = field[:, 0::2]
    odd_planes = field[:, 1::2]
    left_planes = jnp.concatenate([before, odd_planes[:, :-1]], axis=1)
    return 0.125 * (even_planes + 0.5 * (odd_planes + left_planes))


def chebyshev(source, coeff, apply_fn, degree):
    diagonal = 1.0 + 6.0 * coeff[None]
    sigma_ratio = CENTER / HALF_WIDTH
    ratio_old = 1.0 / sigma_ratio
    update = source / (diagonal * CENTER)
    approx = update
    for sweep in range(degree - 1):
        defect = source - apply_fn(approx)
        ratio_new = 1.0 / (2.0 * sigma_ratio - ratio_old)
        update = ratio_new * ratio_old * update + (2.0 * ratio_new / HALF_WIDTH) * (defect / diagonal)
        approx = approx + update
        ratio_old = ratio_new
    return approx


def prolong(extended, rows, cols):
    own_planes = extended[:, :-1]
    mid_planes = 0.5 * (own_planes + extended[:, 1:])
    planes = own_planes.shape[1]
    refined = jnp.stack([own_planes, mid_planes], axis=2).reshape(3, 2 * planes, rows, cols)
    mid_rows = 0.5 * (refined + jnp.roll(refined, -1, 2))
    refined = jnp.stack([refined, mid_rows], axis=3).reshape(3, 2 * planes, 2 * rows, cols)
    mid_cols = 0.5 * (refined + jnp.roll(refined, -1, 3))
    refined = jnp.stack([refined, mid_cols], axis=4).reshape(3, 2 * planes, 2 * rows, 2 * cols)
    return refined.reshape(3, 2 * planes, 4 * rows * cols)


def reference(velocity, forcing, viscosity, coarse_visc):
    fine_rim = jnp.zeros((3, 1, velocity.shape[2]), jnp.float32)
    padded = jnp.concatenate([fine_rim, velocity, fine_rim], axis=1)
    residual = forcing - apply_visc(padded, viscosity, 2 * NY, 2 * NZ)
    crossed = restrict_cross(residual, 2 * NY, 2 * NZ)
    zero_rim = jnp.zeros((3, 1, NY * NZ), jnp.float32)
    coarse_src = restrict_planes(crossed, zero_rim)

    def coarse_apply(approx):
        return apply_visc(jnp.concatenate([zero_rim, approx, zero_rim], axis=1), coarse_visc, NY, NZ)

    coarse_fix = chebyshev(coarse_src, coarse_visc, coarse_apply, DEGREE)
    extended = jnp.concatenate([coarse_fix, zero_rim], axis=1)
    corrected = velocity + prolong(extended, NY, NZ)
    return corrected, coarse_fix
```

```python
import jax
import jax.numpy as jnp
from jax import lax
from jax.experimental import pallas as pl
from jax.experimental.pallas import tpu as pltpu
from jax.sharding import PartitionSpec as P

NY = 32
NZ = 32
DEGREE = 3
LOWER_EIG = 0.15
UPPER_EIG = 1.95
CENTER = 0.5 * (UPPER_EIG + LOWER_EIG)
HALF_WIDTH = 0.5 * (UPPER_EIG - LOWER_EIG)

COMPS = 3
FINE = 4 * NY * NZ
COARSE = NY * NZ
PLANES = 16
HALF = PLANES // 2
LANES = 128
BLOCKS = COARSE // LANES
WIDE = FINE // BLOCKS
TILES = FINE // LANES
F32 = jnp.float32
BF16 = jnp.bfloat16


def fill_restrict(ref):
    fine = lax.broadcasted_iota(jnp.int32, (2 * NZ, LANES), 0)
    lane = lax.broadcasted_iota(jnp.int32, (2 * NZ, LANES), 1)
    apart = (fine - 2 * (lane % NZ) + 2 * NZ) % (2 * NZ)
    cols = jnp.where(apart == 0, 1.0, jnp.where((apart == 1) | (apart == 2 * NZ - 1), 0.5, 0.0))
    for row in range(8):
        away = jnp.abs(2 * (lane // NZ) - row)
        rows = jnp.where(away == 0, 1.0, jnp.where(away == 1, 0.5, 0.0))
        at = slice(2 * NZ * row, 2 * NZ * (row + 1))
        ref[at, :LANES] = (cols * rows).astype(BF16)
        beyond = jnp.where(lane < NZ, 0.5 * cols, 0.0) if row == 7 else jnp.zeros_like(cols)
        ref[at, LANES:] = beyond.astype(BF16)


def fill_prolong(ref):
    coarse = lax.broadcasted_iota(jnp.int32, (NZ, LANES), 0)
    lane = lax.broadcasted_iota(jnp.int32, (NZ, LANES), 1)
    apart = (lane - 2 * coarse + 2 * NZ) % (2 * NZ)
    cols = jnp.where(apart == 0, 1.0, jnp.where((apart == 1) | (apart == 2 * NZ - 1), 0.5, 0.0))
    for row in range(8):
        for part in range(4):
            away = jnp.abs(2 * row - 2 * part - lane // (2 * NZ))
            rows = jnp.where(away == 0, 1.0, jnp.where(away == 1, 0.5, 0.0))
            kept = cols * rows if row < 5 else jnp.zeros_like(cols)
            ref[NZ * row : NZ * (row + 1), tile(part)] = kept.astype(BF16)


def split_dot(left, matrix):
    high = left.astype(BF16)
    low = (left - high.astype(F32)).astype(BF16)
    return jnp.dot(high, matrix, preferred_element_type=F32) + jnp.dot(
        low, matrix, preferred_element_type=F32
    )


def restricted(blocks, matrix):
    sums = split_dot(jnp.concatenate(blocks, axis=0), matrix)
    parts = [sums[PLANES * s : PLANES * (s + 1)] for s in range(BLOCKS)]
    return [parts[s][:, :LANES] + parts[s - 1][:, LANES:] for s in range(BLOCKS)]


def iotas(rows):
    row = lax.broadcasted_iota(jnp.int32, (rows, LANES), 0)
    lane = lax.broadcasted_iota(jnp.int32, (rows, LANES), 1)
    return row, lane


def tile(index):
    return slice(LANES * index, LANES * (index + 1))


def local_kernel(
    v_hbm, f_hbm, c_hbm, cv_ref, s_ref, l_ref, src_ref, w_ref, v_vm, f_vm, c_vm, cross_vm, sems
):
    copies = [pltpu.make_async_copy(c_hbm, c_vm, sems.at[0])]
    for k in range(COMPS):
        copies.append(pltpu.make_async_copy(v_hbm.at[k], v_vm.at[k], sems.at[1 + 2 * k]))
        copies.append(pltpu.make_async_copy(f_hbm.at[k], f_vm.at[k], sems.at[2 + 2 * k]))
    for copy in copies:
        copy.start()

    odd = lax.rem(lax.axis_index("sub"), 2)
    even_device = odd == 0
    s_plane = (PLANES - 1) * (1 - odd)
    l_plane = (PLANES - 1) * odd
    row, lane = iotas(PLANES)
    low_half = lane < 64
    first_col = lane % 64 == 0
    last_col = lane % 64 == 63
    row8, _ = iotas(HALF)
    fill_restrict(w_ref)
    matrix = w_ref[...]

    def send(tile_at, to_right, to_left):
        s_ref[4:8, tile(tile_at)] = jnp.where(even_device, to_right, to_left)[4:8]
        l_ref[4:8, tile(tile_at)] = jnp.where(even_device, to_left, to_right)[4:8]

    for t in range(BLOCKS):
        part = cv_ref[:, tile(t)]
        send(COMPS * BLOCKS + t, pltpu.roll(part, 6, 0), pltpu.roll(part, 4, 0))

    copies[0].wait()
    s_ref[3:4, :] = c_vm[pl.ds(s_plane, 1), :]
    l_ref[3:4, :] = c_vm[pl.ds(l_plane, 1), :]

    for k in range(COMPS):
        copies[1 + 2 * k].wait()
        copies[2 + 2 * k].wait()
        swapped = [pltpu.roll(v_vm[k, :, tile(t)], 64, 1) for t in range(TILES)]
        blocks = []
        for s in range(BLOCKS):
            pieces = []
            for t in range(4 * s, 4 * s + 4):
                x = v_vm[k, :, tile(t)]
                coeff = c_vm[:, tile(t)]
                turned = swapped[t]
                beside = turned + jnp.where(low_half, swapped[t - 1], swapped[(t + 1) % TILES])
                beside += pltpu.roll(jnp.where(last_col, turned, x), 1, 1)
                beside += pltpu.roll(jnp.where(first_col, turned, x), LANES - 1, 1)
                beside += jnp.where(row == 0, 0.0, pltpu.roll(x, 1, 0))
                beside += jnp.where(row == PLANES - 1, 0.0, pltpu.roll(x, PLANES - 1, 0))
                pieces.append(f_vm[k, :, tile(t)] - x + coeff * (beside - 6.0 * x))
            blocks.append(jnp.concatenate(pieces, axis=1))
        crossed = restricted(blocks, matrix)
        for t in range(BLOCKS):
            cross_vm[k * BLOCKS + t] = crossed[t]
        for t in range(BLOCKS):
            evens = cross_vm[k * BLOCKS + t, pl.ds(0, HALF, 2), :]
            odds = 0.0625 * cross_vm[k * BLOCKS + t, pl.ds(1, HALF, 2), :]
            source = 0.125 * evens + odds + jnp.where(row8 == 0, 0.0, pltpu.roll(odds, 1, 0))
            src_ref[k, :, tile(t)] = source
            to_right = jnp.where(row8 == 6, pltpu.roll(odds, 7, 0), pltpu.roll(source, 6, 0))
            send(k * BLOCKS + t, to_right, pltpu.roll(source, 4, 0))
        s_ref[k : k + 1, :] = v_vm[k, pl.ds(s_plane, 1), :]
        l_ref[k : k + 1, :] = v_vm[k, pl.ds(l_plane, 1), :]


def near_sum(tiles, lane):
    ups = [pltpu.roll(x, LANES - NZ, 1) for x in tiles]
    downs = [pltpu.roll(x, NZ, 1) for x in tiles]
    sums = []
    for s, x in enumerate(tiles):
        total = jnp.where(lane < LANES - NZ, ups[s], ups[(s + 1) % BLOCKS])
        total += jnp.where(lane >= NZ, downs[s], downs[s - 1])
        total += pltpu.roll(jnp.where(lane % NZ == NZ - 1, ups[s], x), 1, 1)
        total += pltpu.roll(jnp.where(lane % NZ == 0, downs[s], x), LANES - 1, 1)
        total += pltpu.roll(x, 1, 0) + pltpu.roll(x, PLANES - 1, 0)
        sums.append(total)
    return sums


def finish_kernel(
    v_hbm,
    cv_ref,
    src_ref,
    s_sent,
    l_sent,
    s_got,
    l_got,
    out_hbm,
    fix_ref,
    w_ref,
    q_ref,
    v_vm,
    out_vm,
    mix_vm,
    in_sems,
    out_sems,
):
    loads = [pltpu.make_async_copy(v_hbm.at[k], v_vm.at[k], in_sems.at[k]) for k in range(COMPS)]
    for load in loads:
        load.start()

    even_device = lax.rem(lax.axis_index("sub"), 2) == 0
    _, lane = iotas(PLANES)
    row8, _ = iotas(HALF)
    fill_restrict(w_ref)
    fill_prolong(q_ref)
    matrix = w_ref[...]
    spread = q_ref[...]

    def coupling(sent, got):
        blocks = []
        for s in range(BLOCKS):
            at = slice(WIDE * s, WIDE * (s + 1))
            theirs = got[:, at] * sent[3:4, at]
            ours = sent[:, at] * got[3:4, at]
            blocks.append(jnp.concatenate([theirs, ours], axis=0))
        return restricted(blocks, matrix)

    s_terms = coupling(s_sent, s_got)
    l_terms = coupling(l_sent, l_got)

    def sides(at):
        s_part, l_part = s_got[:, at], l_got[:, at]
        left = jnp.where(even_device, l_part, s_part)
        right = jnp.where(even_device, s_part, l_part)
        above = jnp.where(row8 >= 6, pltpu.roll(left, 2, 0), 0.0)
        below = jnp.where(row8 <= 2, pltpu.roll(right, 4, 0), 0.0)
        return pltpu.roll(left, 2, 0), above + below

    quotients, inverses, inside = [], [], []
    for t in range(BLOCKS):
        _, outer = sides(tile(COMPS * BLOCKS + t))
        coeff = jnp.concatenate([cv_ref[:, tile(t)], outer], axis=0)
        inverse = 1.0 / (1.0 + 6.0 * coeff)
        inverses.append(inverse)
        quotients.append(coeff * inverse)
        inside.append(outer > 0.0)

    sigma = CENTER / HALF_WIDTH
    stores = []
    for k in range(COMPS):
        scaled = []
        for t in range(BLOCKS):
            at = tile(k * BLOCKS + t)
            left_turned, outer = sides(at)
            own_right = pltpu.roll(jnp.where(even_device, s_sent[:, at], l_sent[:, at]), 2, 0)
            left_terms = jnp.where(even_device, l_terms[t], s_terms[t])
            right_terms = jnp.where(even_device, s_terms[t], l_terms[t])
            left_got, left_own = left_terms[k : k + 1], left_terms[HALF + k : HALF + k + 1]
            right_got, right_own = right_terms[k : k + 1], right_terms[HALF + k : HALF + k + 1]
            first = left_turned + (0.125 * left_got + 0.0625 * left_own)
            inner = src_ref[k, :, tile(t)] + jnp.where(row8 == 0, first, 0.0)
            inner += jnp.where(row8 == HALF - 1, 0.0625 * right_got, 0.0)
            after = own_right + (0.0625 * right_got + 0.125 * right_own)
            outer += jnp.where(row8 == 0, after, 0.0)
            outer += jnp.where(row8 == HALF - 1, 0.0625 * left_own, 0.0)
            outer = jnp.where(inside[t], outer, 0.0)
            scaled.append(jnp.concatenate([inner, outer], axis=0) * inverses[t])

        update = [x * (1.0 / CENTER) for x in scaled]
        approx = update
        ratio_old = 1.0 / sigma
        for _ in range(DEGREE - 1):
            ratio_new = 1.0 / (2.0 * sigma - ratio_old)
            keep, gain = ratio_new * ratio_old, 2.0 * ratio_new / HALF_WIDTH
            sums = near_sum(approx, lane)
            update = [
                keep * update[t] + gain * (scaled[t] - approx[t] + quotients[t] * sums[t])
                for t in range(BLOCKS)
            ]
            approx = [approx[t] + update[t] for t in range(BLOCKS)]
            ratio_old = ratio_new

        for t in range(BLOCKS):
            own = approx[t][:HALF]
            fix_ref[k, :, tile(t)] = own
            mix_vm[k * BLOCKS + t, pl.ds(0, HALF, 2), :] = own
            mix_vm[k * BLOCKS + t, pl.ds(1, HALF, 2), :] = 0.5 * (own + pltpu.roll(approx[t], PLANES - 1, 0)[:HALF])
        mixed = [mix_vm[k * BLOCKS + t] for t in range(BLOCKS)]
        pairs = [jnp.concatenate([mixed[s], mixed[(s + 1) % BLOCKS]], axis=1) for s in range(BLOCKS)]
        fine = split_dot(jnp.concatenate(pairs, axis=0), spread)
        loads[k].wait()
        for s in range(BLOCKS):
            at = slice(WIDE * s, WIDE * (s + 1))
            out_vm[k, :, at] = v_vm[k, :, at] + fine[PLANES * s : PLANES * (s + 1)]
        store = pltpu.make_async_copy(out_vm.at[k], out_hbm.at[k], out_sems.at[k])
        store.start()
        stores.append(store)
    for store in stores:
        store.wait()


VMEM = pl.BlockSpec(memory_space=pltpu.VMEM)
ANY = pl.BlockSpec(memory_space=pl.ANY)
LIMIT = 16 * 2**20


def shards(velocity, forcing, viscosity, coarse_visc):
    message = jax.ShapeDtypeStruct((8, FINE), F32)
    s_sent, l_sent, source = pl.pallas_call(
        local_kernel,
        out_shape=(message, message, jax.ShapeDtypeStruct((COMPS, HALF, COARSE), F32)),
        in_specs=[ANY, ANY, ANY, VMEM],
        out_specs=(VMEM, VMEM, VMEM),
        scratch_shapes=[
            pltpu.VMEM((WIDE, 2 * LANES), BF16),
            pltpu.VMEM((COMPS, PLANES, FINE), F32),
            pltpu.VMEM((COMPS, PLANES, FINE), F32),
            pltpu.VMEM((PLANES, FINE), F32),
            pltpu.VMEM((COMPS * BLOCKS, PLANES, LANES), F32),
            pltpu.SemaphoreType.DMA((1 + 2 * COMPS,)),
        ],
        compiler_params=pltpu.CompilerParams(vmem_limit_bytes=LIMIT),
    )(velocity, forcing, viscosity, coarse_visc)

    axes = ("grp", "sub")
    count = lax.axis_size(axes)
    far = [(i, i + 1) for i in range(1, count - 1, 2)]
    near = [(i, i + 1) for i in range(0, count, 2)]
    l_got = lax.ppermute(l_sent, axes, far + [(j, i) for i, j in far])
    s_got = lax.ppermute(s_sent, axes, near + [(j, i) for i, j in near])

    return pl.pallas_call(
        finish_kernel,
        out_shape=(
            jax.ShapeDtypeStruct(velocity.shape, F32),
            jax.ShapeDtypeStruct((COMPS, HALF, COARSE), F32),
        ),
        in_specs=[ANY] + [VMEM] * 6,
        out_specs=(ANY, VMEM),
        scratch_shapes=[
            pltpu.VMEM((WIDE, 2 * LANES), BF16),
            pltpu.VMEM((2 * LANES, WIDE), BF16),
            pltpu.VMEM((COMPS, PLANES, FINE), F32),
            pltpu.VMEM((COMPS, PLANES, FINE), F32),
            pltpu.VMEM((COMPS * BLOCKS, PLANES, LANES), F32),
            pltpu.SemaphoreType.DMA((COMPS,)),
            pltpu.SemaphoreType.DMA((COMPS,)),
        ],
        compiler_params=pltpu.CompilerParams(vmem_limit_bytes=LIMIT),
    )(velocity, coarse_visc, source, s_sent, l_sent, s_got, l_got)


def solution(mesh):
    return jax.shard_map(
        shards,
        mesh=mesh,
        in_specs=(
            P(None, ("grp", "sub"), None),
            P(None, ("grp", "sub"), None),
            P(("grp", "sub"), None),
            P(("grp", "sub"), None),
        ),
        out_specs=(P(None, ("grp", "sub"), None), P(None, ("grp", "sub"), None)),
        check_vma=False,
    )
```

```python
import jax
import jax.numpy as jnp
from jax import lax
from jax.experimental import pallas as pl
from jax.experimental.pallas import tpu as pltpu
from jax.sharding import PartitionSpec as P

NY = 32
NZ = 32
DEGREE = 3
LOWER_EIG = 0.15
UPPER_EIG = 1.95
CENTER = 0.5 * (UPPER_EIG + LOWER_EIG)
HALF_WIDTH = 0.5 * (UPPER_EIG - LOWER_EIG)

COMPS = 3
FINE = 4 * NY * NZ
COARSE = NY * NZ
PLANES = 16
HALF = PLANES // 2
LANES = 128
BLOCKS = COARSE // LANES
WIDE = FINE // BLOCKS
TILES = FINE // LANES
F32 = jnp.float32
BF16 = jnp.bfloat16


def tile(index):
    return slice(LANES * index, LANES * (index + 1))


def fill_restrict(ref):
    fine = lax.broadcasted_iota(jnp.int32, (2 * NZ, LANES), 0)
    lane = lax.broadcasted_iota(jnp.int32, (2 * NZ, LANES), 1)
    apart = (fine - 2 * (lane % NZ) + 2 * NZ) % (2 * NZ)
    cols = jnp.where(apart == 0, 1.0, jnp.where((apart == 1) | (apart == 2 * NZ - 1), 0.5, 0.0))
    for row in range(8):
        away = jnp.abs(2 * (lane // NZ) - row)
        rows = jnp.where(away == 0, 1.0, jnp.where(away == 1, 0.5, 0.0))
        at = slice(2 * NZ * row, 2 * NZ * (row + 1))
        ref[at, :LANES] = (cols * rows).astype(BF16)
        beyond = jnp.where(lane < NZ, 0.5 * cols, 0.0) if row == 7 else jnp.zeros_like(cols)
        ref[at, LANES:] = beyond.astype(BF16)


def fill_prolong(ref):
    coarse = lax.broadcasted_iota(jnp.int32, (NZ, LANES), 0)
    lane = lax.broadcasted_iota(jnp.int32, (NZ, LANES), 1)
    apart = (lane - 2 * coarse + 2 * NZ) % (2 * NZ)
    cols = jnp.where(apart == 0, 1.0, jnp.where((apart == 1) | (apart == 2 * NZ - 1), 0.5, 0.0))
    for row in range(8):
        for part in range(4):
            away = jnp.abs(2 * row - 2 * part - lane // (2 * NZ))
            rows = jnp.where(away == 0, 1.0, jnp.where(away == 1, 0.5, 0.0))
            kept = cols * rows if row < 5 else jnp.zeros_like(cols)
            ref[NZ * row : NZ * (row + 1), tile(part)] = kept.astype(BF16)


def split_dot(left, matrix):
    high = left.astype(BF16)
    low = (left - high.astype(F32)).astype(BF16)
    return jnp.dot(high, matrix, preferred_element_type=F32) + jnp.dot(
        low, matrix, preferred_element_type=F32
    )


def iotas(rows):
    row = lax.broadcasted_iota(jnp.int32, (rows, LANES), 0)
    lane = lax.broadcasted_iota(jnp.int32, (rows, LANES), 1)
    return row, lane


def eight(index):
    return slice(8 * index, 8 * (index + 1))


def local_kernel(
    v_hbm,
    f_hbm,
    c_hbm,
    cv_hbm,
    right_ref,
    left_ref,
    src_ref,
    v_ref,
    cv_ref,
    w_ref,
    q_ref,
    f_vm,
    c_vm,
    cross_vm,
    sems,
):
    copies = [pltpu.make_async_copy(c_hbm, c_vm, sems.at[0])]
    for k in range(COMPS):
        copies.append(pltpu.make_async_copy(v_hbm.at[k], v_ref.at[k], sems.at[1 + 2 * k]))
        copies.append(pltpu.make_async_copy(f_hbm.at[k], f_vm.at[k], sems.at[2 + 2 * k]))
    copies.append(pltpu.make_async_copy(cv_hbm, cv_ref, sems.at[1 + 2 * COMPS]))
    for copy in copies:
        copy.start()

    row, lane = iotas(PLANES)
    low_half = lane < 64
    first_col = lane % 64 == 0
    last_col = lane % 64 == 63
    fill_restrict(w_ref)
    fill_prolong(q_ref)
    matrix = w_ref[...]

    def packed_planes(slab, source):
        for part in range(4):
            left_ref[slab, :, tile(part)] = source[0, pl.ds(8 * part, 8, 32), :]
            right_ref[slab, :, tile(part)] = source[1, pl.ds(8 * part + 7, 8, 32), :]

    copies[0].wait()
    packed_planes(COMPS, c_vm)

    for k in range(COMPS):
        copies[1 + 2 * k].wait()
        copies[2 + 2 * k].wait()

        def planes_of(ref, t):
            return jnp.concatenate([ref[0, eight(t), :], ref[1, eight(t), :]], axis=0)

        values = [planes_of(v_ref.at[k], t) for t in range(TILES)]
        swapped = [pltpu.roll(x, 64, 1) for x in values]
        blocks = []
        for s in range(BLOCKS):
            pieces = []
            for t in range(4 * s, 4 * s + 4):
                x, turned = values[t], swapped[t]
                beside = turned + jnp.where(low_half, swapped[t - 1], swapped[(t + 1) % TILES])
                beside += pltpu.roll(jnp.where(last_col, turned, x), 1, 1)
                beside += pltpu.roll(jnp.where(first_col, turned, x), LANES - 1, 1)
                beside += jnp.where(row == 0, 0.0, pltpu.roll(x, 1, 0))
                beside += jnp.where(row == PLANES - 1, 0.0, pltpu.roll(x, PLANES - 1, 0))
                pieces.append(
                    planes_of(f_vm.at[k], t) - x + planes_of(c_vm, t) * (beside - 6.0 * x)
                )
            blocks.append(jnp.concatenate(pieces, axis=1))
        sums = split_dot(jnp.concatenate(blocks, axis=0), matrix)
        parts = [sums[PLANES * s : PLANES * (s + 1)] for s in range(BLOCKS)]
        for s in range(BLOCKS):
            crossed = parts[s][:, :LANES] + parts[s - 1][:, LANES:]
            cross_vm[k, PLANES * s : PLANES * (s + 1), :] = crossed
        planes = [cross_vm[k, pl.ds(p, 8, PLANES), :] for p in range(PLANES)]
        half_odds = [0.0625 * planes[2 * j + 1] for j in range(HALF)]
        sources = []
        for j in range(HALF):
            source = 0.125 * planes[2 * j] + half_odds[j]
            if j > 0:
                source += half_odds[j - 1]
            src_ref[k, eight(j), :] = source
            sources.append(source)
        for j in range(3):
            left_ref[4 + j, :, tile(k)] = sources[j]
            right_ref[4 + j, :, tile(k)] = (sources[6:] + half_odds[-1:])[j]
        packed_planes(k, v_ref.at[k])

    copies[-1].wait()
    for j in range(3):
        left_ref[4 + j, :, tile(COMPS)] = cv_ref[pl.ds(j, 8, 8), :]
        right_ref[4 + j, :, tile(COMPS)] = cv_ref[pl.ds(min(6 + j, 7), 8, 8), :]


def finish_kernel(
    v_ref,
    cv_ref,
    src_ref,
    right_sent,
    left_sent,
    right_got,
    left_got,
    w_ref,
    q_ref,
    out_hbm,
    fix_ref,
    out_vm,
    mix_vm,
    sems,
):
    _, lane = iotas(8)
    kept_up = lane < LANES - NZ
    kept_down = lane >= NZ
    first_col = lane % NZ == 0
    last_col = lane % NZ == NZ - 1

    rows = []
    for sent, got in ((left_sent, right_got), (right_sent, left_got)):
        rows += [got[k] * sent[COMPS] for k in range(COMPS)]
        rows += [sent[k] * got[COMPS] for k in range(COMPS)]
    sums = split_dot(jnp.concatenate(rows, axis=0), w_ref[...])
    terms = []
    for part in range(len(rows)):
        mine = sums[eight(part)]
        terms.append(mine[:, :LANES] + pltpu.roll(mine[:, LANES:], 1, 0))

    first, last = -2, HALF + 2
    inverse, quotient = {}, {}
    for j in range(first, last + 1):
        if j < 0:
            coeff = right_got[6 + j, :, tile(COMPS)]
        elif j < HALF:
            coeff = cv_ref[pl.ds(j, 8, 8), :]
        else:
            coeff = left_got[4 + j - HALF, :, tile(COMPS)]
        if j == HALF:
            inside = coeff > 0.0
        inverse[j] = 1.0 / (1.0 + 6.0 * coeff)
        quotient[j] = coeff * inverse[j]

    def near_sum(planes, j):
        x = planes[j]
        up = pltpu.roll(x, LANES - NZ, 1)
        down = pltpu.roll(x, NZ, 1)
        total = planes[j - 1] + planes[j + 1]
        total += jnp.where(kept_up, up, pltpu.roll(up, 7, 0))
        total += jnp.where(kept_down, down, pltpu.roll(down, 1, 0))
        total += pltpu.roll(jnp.where(last_col, up, x), 1, 1)
        total += pltpu.roll(jnp.where(first_col, down, x), LANES - 1, 1)
        return total

    sigma = CENTER / HALF_WIDTH
    stores = []
    for k in range(COMPS):
        at = tile(k)
        left_theirs, left_ours = terms[k], terms[COMPS + k]
        right_theirs, right_ours = terms[2 * COMPS + k], terms[3 * COMPS + k]
        source = {j: src_ref[k, eight(j), :] for j in range(HALF)}
        source[-2] = right_got[4, :, at]
        source[-1] = right_got[5, :, at] + 0.0625 * left_ours
        source[0] += right_got[6, :, at] + (0.125 * left_theirs + 0.0625 * left_ours)
        source[HALF - 1] += 0.0625 * right_theirs
        after = right_sent[6, :, at] + left_got[4, :, at] + (0.0625 * right_theirs + 0.125 * right_ours)
        source[HALF] = jnp.where(inside, after, 0.0)
        source[HALF + 1] = left_got[5, :, at]
        source[HALF + 2] = left_got[6, :, at]

        scaled = {j: source[j] * inverse[j] for j in source}
        update = {j: x * (1.0 / CENTER) for j, x in scaled.items()}
        approx = update
        ratio_old = 1.0 / sigma
        for sweep in range(1, DEGREE):
            ratio_new = 1.0 / (2.0 * sigma - ratio_old)
            keep, gain = ratio_new * ratio_old, 2.0 * ratio_new / HALF_WIDTH
            inner = range(first + sweep, last - sweep + 1)
            update = {
                j: keep * update[j]
                + gain * (scaled[j] - approx[j] + quotient[j] * near_sum(approx, j))
                for j in inner
            }
            approx = {j: approx[j] + update[j] for j in inner}
            ratio_old = ratio_new

        for j in range(HALF):
            fix_ref[k, pl.ds(j, 8, 8), :] = approx[j]
            mix_vm[k, eight(2 * j), :] = approx[j]
            mix_vm[k, eight(2 * j + 1), :] = 0.5 * (approx[j] + approx[j + 1])
        mixed = [
            [mix_vm[k, pl.ds(64 * h + s, 8, 8), :] for s in range(BLOCKS)] for h in range(2)
        ]
        left = [
            jnp.concatenate([mixed[h][s], mixed[h][(s + 1) % BLOCKS]], axis=1)
            for h in range(2)
            for s in range(BLOCKS)
        ]
        fine = split_dot(jnp.concatenate(left, axis=0), q_ref[...])
        for h in range(2):
            for t in range(TILES):
                add = fine[eight(BLOCKS * h + t // 4), tile(t % 4)]
                out_vm[k, h, eight(t), :] = v_ref[k, h, eight(t), :] + add
        store = pltpu.make_async_copy(out_vm.at[k], out_hbm.at[k], sems.at[k])
        store.start()
        stores.append(store)
    for store in stores:
        store.wait()


VMEM = pl.BlockSpec(memory_space=pltpu.VMEM)
HBM = pl.BlockSpec(memory_space=pltpu.HBM)
LIMIT = 16 * 2**20
FINE_TILED = (2, 8 * TILES, LANES)


def fine_tiled(field):
    lead = field.shape[:-2]
    split = field.reshape(lead + (2, 8, TILES, LANES))
    return jnp.swapaxes(split, -3, -2).reshape(lead + FINE_TILED)


def pinned(field):
    return pltpu.with_memory_space_constraint(fine_tiled(field), pltpu.HBM)


def shards(velocity, forcing, viscosity, coarse_visc):
    coeffs = jnp.swapaxes(coarse_visc.reshape(HALF, BLOCKS, LANES), 0, 1).reshape(8 * HALF, LANES)
    coeffs = pltpu.with_memory_space_constraint(coeffs, pltpu.HBM)
    message = jax.ShapeDtypeStruct((7, 8, WIDE), F32)
    fine = jax.ShapeDtypeStruct((COMPS,) + FINE_TILED, F32)
    coarse = jax.ShapeDtypeStruct((COMPS, 8 * HALF, LANES), F32)
    right_sent, left_sent, source, kept, coeffs, restrict, prolong = pl.pallas_call(
        local_kernel,
        out_shape=(
            message,
            message,
            coarse,
            fine,
            jax.ShapeDtypeStruct((8 * HALF, LANES), F32),
            jax.ShapeDtypeStruct((WIDE, 2 * LANES), BF16),
            jax.ShapeDtypeStruct((2 * LANES, WIDE), BF16),
        ),
        in_specs=[HBM] * 4,
        out_specs=(VMEM,) * 7,
        scratch_shapes=[
            pltpu.VMEM((COMPS,) + FINE_TILED, F32),
            pltpu.VMEM(FINE_TILED, F32),
            pltpu.VMEM((COMPS, 8 * PLANES, LANES), F32),
            pltpu.SemaphoreType.DMA((2 + 2 * COMPS,)),
        ],
        compiler_params=pltpu.CompilerParams(vmem_limit_bytes=LIMIT),
    )(pinned(velocity), pinned(forcing), pinned(viscosity), coeffs)

    axes = ("grp", "sub")
    count = lax.axis_size(axes)
    forward = [(i, i + 1) for i in range(count - 1)]
    right_got = lax.ppermute(right_sent, axes, forward)
    left_got = lax.ppermute(left_sent, axes, [(j, i) for i, j in forward])

    corrected, fix = pl.pallas_call(
        finish_kernel,
        out_shape=(fine, coarse),
        in_specs=[VMEM] * 9,
        out_specs=(HBM, VMEM),
        scratch_shapes=[
            pltpu.VMEM((COMPS,) + FINE_TILED, F32),
            pltpu.VMEM((COMPS, 8 * PLANES, LANES), F32),
            pltpu.SemaphoreType.DMA((COMPS,)),
        ],
        compiler_params=pltpu.CompilerParams(vmem_limit_bytes=LIMIT),
    )(kept, coeffs, source, right_sent, left_sent, right_got, left_got, restrict, prolong)
    corrected = corrected.reshape(COMPS, 2, TILES, 8, LANES)
    fix = fix.reshape(COMPS, BLOCKS, HALF, LANES)
    return (
        jnp.swapaxes(corrected, 2, 3).reshape(velocity.shape),
        jnp.swapaxes(fix, 1, 2).reshape(COMPS, HALF, COARSE),
    )


def solution(mesh):
    return jax.shard_map(
        shards,
        mesh=mesh,
        in_specs=(
            P(None, ("grp", "sub"), None),
            P(None, ("grp", "sub"), None),
            P(("grp", "sub"), None),
            P(("grp", "sub"), None),
        ),
        out_specs=(P(None, ("grp", "sub"), None), P(None, ("grp", "sub"), None)),
        check_vma=False,
    )
```

```python
import jax
import jax.numpy as jnp
from jax import lax
from jax.experimental import pallas as pl
from jax.experimental.pallas import tpu as pltpu
from jax.sharding import PartitionSpec as P

NY = 32
NZ = 32
DEGREE = 3
LOWER_EIG = 0.15
UPPER_EIG = 1.95
CENTER = 0.5 * (UPPER_EIG + LOWER_EIG)
HALF_WIDTH = 0.5 * (UPPER_EIG - LOWER_EIG)

COMPS = 3
FINE = 4 * NY * NZ
COARSE = NY * NZ
PLANES = 16
HALF = PLANES // 2
LANES = 128
BLOCKS = COARSE // LANES
WIDE = FINE // BLOCKS
TILES = FINE // LANES
F32 = jnp.float32
BF16 = jnp.bfloat16


def tile(index):
    return slice(LANES * index, LANES * (index + 1))


def fill_restrict(ref):
    fine = lax.broadcasted_iota(jnp.int32, (2 * NZ, LANES), 0)
    lane = lax.broadcasted_iota(jnp.int32, (2 * NZ, LANES), 1)
    apart = (fine - 2 * (lane % NZ) + 2 * NZ) % (2 * NZ)
    cols = jnp.where(apart == 0, 1.0, jnp.where((apart == 1) | (apart == 2 * NZ - 1), 0.5, 0.0))
    for row in range(8):
        away = jnp.abs(2 * (lane // NZ) - row)
        rows = jnp.where(away == 0, 1.0, jnp.where(away == 1, 0.5, 0.0))
        at = slice(2 * NZ * row, 2 * NZ * (row + 1))
        ref[at, :LANES] = (cols * rows).astype(BF16)
        beyond = jnp.where(lane < NZ, 0.5 * cols, 0.0) if row == 7 else jnp.zeros_like(cols)
        ref[at, LANES:] = beyond.astype(BF16)


def fill_prolong(ref):
    coarse = lax.broadcasted_iota(jnp.int32, (NZ, LANES), 0)
    lane = lax.broadcasted_iota(jnp.int32, (NZ, LANES), 1)
    apart = (lane - 2 * coarse + 2 * NZ) % (2 * NZ)
    cols = jnp.where(apart == 0, 1.0, jnp.where((apart == 1) | (apart == 2 * NZ - 1), 0.5, 0.0))
    for row in range(8):
        for part in range(4):
            away = jnp.abs(2 * row - 2 * part - lane // (2 * NZ))
            rows = jnp.where(away == 0, 1.0, jnp.where(away == 1, 0.5, 0.0))
            kept = cols * rows if row < 5 else jnp.zeros_like(cols)
            ref[NZ * row : NZ * (row + 1), tile(part)] = kept.astype(BF16)


def split_dot(left, matrix):
    high = left.astype(BF16)
    low = (left - high.astype(F32)).astype(BF16)
    return jnp.dot(high, matrix, preferred_element_type=F32) + jnp.dot(
        low, matrix, preferred_element_type=F32
    )


def iotas(rows):
    row = lax.broadcasted_iota(jnp.int32, (rows, LANES), 0)
    lane = lax.broadcasted_iota(jnp.int32, (rows, LANES), 1)
    return row, lane


def eight(index):
    return slice(8 * index, 8 * (index + 1))


def place():
    at = lax.axis_index("sub")
    return at, lax.rem(at, 2), at < lax.axis_size("sub") - 2


def local_half(h, v_ref, f_ref, c_ref, w_ref, cross_ref, ready):
    row, lane = iotas(8)
    low_half = lane < 64
    first_col = lane % 64 == 0
    last_col = lane % 64 == 63
    upper = h == 1
    matrix = w_ref[...]
    for k in range(COMPS):
        ready(k)
        values = [v_ref[k, h, eight(t), :] for t in range(TILES)]
        swapped = [pltpu.roll(x, 64, 1) for x in values]
        blocks = []
        for s in range(BLOCKS):
            pieces = []
            for t in range(4 * s, 4 * s + 4):
                x, turned = values[t], swapped[t]
                edge = v_ref[k, 1 - h, pl.ds(8 * t + 7 * h, 1), :]
                beside = turned + jnp.where(low_half, swapped[t - 1], swapped[(t + 1) % TILES])
                beside += pltpu.roll(jnp.where(last_col, turned, x), 1, 1)
                beside += pltpu.roll(jnp.where(first_col, turned, x), LANES - 1, 1)
                beside += jnp.where(row == 0, jnp.where(upper, edge, 0.0), pltpu.roll(x, 1, 0))
                beside += jnp.where(row == 7, jnp.where(upper, 0.0, edge), pltpu.roll(x, 7, 0))
                coeff = c_ref[h, eight(t), :]
                pieces.append(f_ref[k, h, eight(t), :] - x + coeff * (beside - 6.0 * x))
            blocks.append(jnp.concatenate(pieces, axis=1))
        sums = split_dot(jnp.concatenate(blocks, axis=0), matrix)
        parts = [sums[eight(s)] for s in range(BLOCKS)]
        for s in range(BLOCKS):
            cross_ref[k, h, eight(s), :] = parts[s][:, :LANES] + parts[s - 1][:, LANES:]


def write_message(h, ref, v_ref, c_ref, cv_ref, cross_ref):
    upper = h == 1
    for part in range(4):
        rows = pl.ds(8 * part + 7 * h, 8, 32)
        ref[COMPS, :, tile(part)] = c_ref[h, rows, :]
        for k in range(COMPS):
            ref[k, :, tile(part)] = v_ref[k, h, rows, :]
    for j in range(3):
        ref[4 + j, :, tile(COMPS)] = cv_ref[pl.ds(j + h * min(6, 7 - j), 8, 8), :]
    for k in range(COMPS):
        planes = [cross_ref[k, h, pl.ds(i, 8, 8), :] for i in range(8)]

        def source(i):
            return 0.125 * planes[i] + 0.0625 * (planes[i - 1] + planes[i + 1])

        middle = source(4)
        first = 0.125 * planes[0] + 0.0625 * planes[1]
        ref[4, :, tile(k)] = jnp.where(upper, middle, first)
        ref[5, :, tile(k)] = jnp.where(upper, source(6), source(2))
        ref[6, :, tile(k)] = jnp.where(upper, 0.0625 * planes[7], middle)


def local_kernel(
    v_hbm,
    f_hbm,
    c_hbm,
    cv_hbm,
    early_ref,
    middle_ref,
    cross_ref,
    v_ref,
    f_ref,
    c_ref,
    cv_ref,
    w_ref,
    q_ref,
    sems,
):
    _, h, early = place()
    copies = [pltpu.make_async_copy(c_hbm.at[h], c_ref.at[h], sems.at[0])]
    for k in range(COMPS):
        copies.append(pltpu.make_async_copy(v_hbm.at[k], v_ref.at[k], sems.at[1 + 2 * k]))
        copies.append(pltpu.make_async_copy(f_hbm.at[k, h], f_ref.at[k, h], sems.at[2 + 2 * k]))
    copies.append(pltpu.make_async_copy(cv_hbm, cv_ref, sems.at[7]))
    copies.append(pltpu.make_async_copy(c_hbm.at[1 - h], c_ref.at[1 - h], sems.at[8]))
    for k in range(COMPS):
        copies.append(
            pltpu.make_async_copy(f_hbm.at[k, 1 - h], f_ref.at[k, 1 - h], sems.at[9 + k])
        )
    for copy in copies:
        copy.start()
    fill_restrict(w_ref)
    fill_prolong(q_ref)

    def ready(k):
        if k == 0:
            copies[0].wait()
        copies[1 + 2 * k].wait()
        copies[2 + 2 * k].wait()

    local_half(h, v_ref, f_ref, c_ref, w_ref, cross_ref, ready)
    for copy in copies[7:]:
        copy.wait()
    write_message(h, middle_ref, v_ref, c_ref, cv_ref, cross_ref)

    @pl.when(early)
    def _():
        local_half(1 - h, v_ref, f_ref, c_ref, w_ref, cross_ref, lambda k: None)
        write_message(1 - h, early_ref, v_ref, c_ref, cv_ref, cross_ref)


def late_kernel(
    after, early_in, cross_in, v_ref, f_ref, c_ref, cv_ref, w_ref, early_ref, cross_ref
):
    del after
    _, h, early = place()
    cross_ref[:, h] = cross_in[:, h]

    @pl.when(early)
    def _():
        early_ref[...] = early_in[...]
        cross_ref[:, 1 - h] = cross_in[:, 1 - h]

    @pl.when(jnp.logical_not(early))
    def _():
        local_half(1 - h, v_ref, f_ref, c_ref, w_ref, cross_ref, lambda k: None)
        write_message(1 - h, early_ref, v_ref, c_ref, cv_ref, cross_ref)


def finish_half(h, sent, got, cross_ref, v_ref, cv_ref, w_ref, q_ref, mix_vm, out_vm, out_hbm, sems, keep_fix):
    _, lane = iotas(8)
    kept_up = lane < LANES - NZ
    kept_down = lane >= NZ
    first_col = lane % NZ == 0
    last_col = lane % NZ == NZ - 1
    whole = slice(0, WIDE)

    their_coeff, own_coeff = got(COMPS, whole), sent(COMPS, whole)
    rows = [got(k, whole) * own_coeff for k in range(COMPS)]
    rows += [sent(k, whole) * their_coeff for k in range(COMPS)]
    sums = split_dot(jnp.concatenate(rows, axis=0), w_ref[...])
    terms = []
    for part in range(2 * COMPS):
        mine = sums[eight(part)]
        terms.append(mine[:, :LANES] + pltpu.roll(mine[:, LANES:], 1, 0))

    first = 4 * h - 2
    last = first + 8
    inverse, quotient = {}, {}
    for j in range(first, last + 1):
        if j < 0:
            coeff = got(6 + j, tile(COMPS))
        elif j < HALF:
            coeff = cv_ref[pl.ds(j, 8, 8), :]
        else:
            coeff = got(4 + j - HALF, tile(COMPS))
        if j == HALF:
            inside = coeff > 0.0
        inverse[j] = 1.0 / (1.0 + 6.0 * coeff)
        quotient[j] = coeff * inverse[j]

    def near_sum(planes, j):
        x = planes[j]
        up = pltpu.roll(x, LANES - NZ, 1)
        down = pltpu.roll(x, NZ, 1)
        total = planes[j - 1] + planes[j + 1]
        total += jnp.where(kept_up, up, pltpu.roll(up, 7, 0))
        total += jnp.where(kept_down, down, pltpu.roll(down, 1, 0))
        total += pltpu.roll(jnp.where(last_col, up, x), 1, 1)
        total += pltpu.roll(jnp.where(first_col, down, x), LANES - 1, 1)
        return total

    sigma = CENTER / HALF_WIDTH
    stores = []
    for k in range(COMPS):
        at = tile(k)
        theirs, ours = terms[k], terms[COMPS + k]

        def crossed(p):
            return cross_ref[k, p // 8, pl.ds(p % 8, 8, 8), :]

        source = {}
        for j in range(max(first, 0), min(last, HALF - 1) + 1):
            beside = crossed(2 * j + 1)
            if j > 0:
                beside += crossed(2 * j - 1)
            source[j] = 0.125 * crossed(2 * j) + 0.0625 * beside
        if h == 0:
            source[-2] = got(4, at)
            source[-1] = got(5, at) + 0.0625 * ours
            source[0] += got(6, at) + (0.125 * theirs + 0.0625 * ours)
        else:
            source[HALF - 1] += 0.0625 * theirs
            after = sent(6, at) + got(4, at) + (0.0625 * theirs + 0.125 * ours)
            source[HALF] = jnp.where(inside, after, 0.0)
            source[HALF + 1] = got(5, at)
            source[HALF + 2] = got(6, at)

        scaled = {j: source[j] * inverse[j] for j in source}
        update = {j: x * (1.0 / CENTER) for j, x in scaled.items()}
        approx = update
        ratio_old = 1.0 / sigma
        for sweep in range(1, DEGREE):
            ratio_new = 1.0 / (2.0 * sigma - ratio_old)
            keep, gain = ratio_new * ratio_old, 2.0 * ratio_new / HALF_WIDTH
            inner = range(first + sweep, last - sweep + 1)
            update = {
                j: keep * update[j]
                + gain * (scaled[j] - approx[j] + quotient[j] * near_sum(approx, j))
                for j in inner
            }
            approx = {j: approx[j] + update[j] for j in inner}
            ratio_old = ratio_new

        for i in range(4):
            here, after = approx[4 * h + i], approx[4 * h + i + 1]
            keep_fix(k, i, here)
            mix_vm[k, eight(2 * i), :] = here
            mix_vm[k, eight(2 * i + 1), :] = 0.5 * (here + after)
        mixed = [mix_vm[k, pl.ds(s, 8, 8), :] for s in range(BLOCKS)]
        left = [
            jnp.concatenate([mixed[s], mixed[(s + 1) % BLOCKS]], axis=1) for s in range(BLOCKS)
        ]
        fine = split_dot(jnp.concatenate(left, axis=0), q_ref[...])
        for t in range(TILES):
            add = fine[eight(t // 4), tile(t % 4)]
            out_vm[k, h, eight(t), :] = v_ref[k, h, eight(t), :] + add
        store = pltpu.make_async_copy(out_vm.at[k, h], out_hbm.at[k, h], sems.at[k, h])
        store.start()
        stores.append(store)
    return stores


def upper_kernel(
    early_in,
    middle_in,
    early_got,
    cross_ref,
    v_ref,
    cv_ref,
    w_ref,
    q_ref,
    middle_ref,
    out_hbm,
    fix_ref,
    mix_vm,
    out_vm,
    sems,
):
    del middle_in, middle_ref
    at, _, _ = place()

    @pl.when(at == 0)
    def _():
        def keep_fix(k, i, plane):
            fix_ref[k, eight(i), :] = plane

        stores = finish_half(
            1,
            lambda slab, lanes: early_in[slab, :, lanes],
            lambda slab, lanes: early_got[slab, :, lanes],
            cross_ref,
            v_ref,
            cv_ref,
            w_ref,
            q_ref,
            mix_vm,
            out_vm,
            out_hbm,
            sems,
            keep_fix,
        )
        for store in stores:
            store.wait()


def lower_kernel(
    out_in,
    upper_fix,
    middle_sent,
    middle_got,
    cross_ref,
    v_ref,
    cv_ref,
    w_ref,
    q_ref,
    out_hbm,
    fix_hbm,
    mix_vm,
    out_vm,
    sems,
    fix_vm,
    fix_sem,
):
    del out_in
    at, _, _ = place()

    @pl.when(at == 0)
    def _():
        def keep_fix(k, i, plane):
            fix_vm[k, pl.ds(i, 8, 8), :] = plane

        for k in range(COMPS):
            for i in range(4):
                fix_vm[k, pl.ds(4 + i, 8, 8), :] = upper_fix[k, eight(i), :]
        stores = finish_half(
            0,
            lambda slab, lanes: middle_sent[slab, :, lanes],
            lambda slab, lanes: middle_got[slab, :, lanes],
            cross_ref,
            v_ref,
            cv_ref,
            w_ref,
            q_ref,
            mix_vm,
            out_vm,
            out_hbm,
            sems,
            keep_fix,
        )
        fix_copy = pltpu.make_async_copy(fix_vm, fix_hbm, fix_sem)
        fix_copy.start()
        for store in stores:
            store.wait()
        fix_copy.wait()


def finish_kernel(
    out_in,
    fix_in,
    early_sent,
    middle_sent,
    middle_got,
    early_got,
    late_got,
    cross_ref,
    v_ref,
    cv_ref,
    w_ref,
    q_ref,
    out_hbm,
    fix_hbm,
    mix_vm,
    out_vm,
    sems,
    fix_vm,
    fix_sem,
):
    del out_in, fix_in
    at, h, early = place()
    even = h == 0

    def outer_got(slab, lanes):
        return jnp.where(early, early_got[slab, :, lanes], late_got[slab, :, lanes])

    def left_sent(slab, lanes):
        return jnp.where(even, middle_sent[slab, :, lanes], early_sent[slab, :, lanes])

    def left_got(slab, lanes):
        return jnp.where(even, middle_got[slab, :, lanes], outer_got(slab, lanes))

    def right_sent(slab, lanes):
        return jnp.where(even, early_sent[slab, :, lanes], middle_sent[slab, :, lanes])

    def right_got(slab, lanes):
        return jnp.where(even, outer_got(slab, lanes), middle_got[slab, :, lanes])

    def half(which, sent, got):
        def keep_fix(k, i, plane):
            fix_vm[k, pl.ds(4 * which + i, 8, 8), :] = plane

        refs = (cross_ref, v_ref, cv_ref, w_ref, q_ref, mix_vm, out_vm, out_hbm, sems, keep_fix)
        return finish_half(which, sent, got, *refs)

    @pl.when(at != 0)
    def _():
        stores = half(0, left_sent, left_got) + half(1, right_sent, right_got)
        fix_copy = pltpu.make_async_copy(fix_vm, fix_hbm, fix_sem)
        fix_copy.start()
        for store in stores:
            store.wait()
        fix_copy.wait()


VMEM = pl.BlockSpec(memory_space=pltpu.VMEM)
HBM = pl.BlockSpec(memory_space=pltpu.HBM)
ANY = pl.BlockSpec(memory_space=pl.ANY)
PARAMS = pltpu.CompilerParams(vmem_limit_bytes=16 * 2**20)
FINE_TILED = (2, 8 * TILES, LANES)


def fine_tiled(field):
    lead = field.shape[:-2]
    split = field.reshape(lead + (2, 8, TILES, LANES))
    return jnp.swapaxes(split, -3, -2).reshape(lead + FINE_TILED)


def pinned(field):
    return pltpu.with_memory_space_constraint(field, pltpu.HBM)


def shards(velocity, forcing, viscosity, coarse_visc):
    coeffs = jnp.swapaxes(coarse_visc.reshape(HALF, BLOCKS, LANES), 0, 1).reshape(8 * HALF, LANES)
    message = jax.ShapeDtypeStruct((7, 8, WIDE), F32)
    fine = jax.ShapeDtypeStruct((COMPS,) + FINE_TILED, F32)
    coarse = jax.ShapeDtypeStruct((COMPS, 8 * HALF, LANES), F32)
    crosses = jax.ShapeDtypeStruct((COMPS, 2, 8 * 8, LANES), F32)
    early, middle, cross, v_kept, f_kept, c_kept, cv_kept, restrict, prolong = pl.pallas_call(
        local_kernel,
        out_shape=(
            message,
            message,
            crosses,
            fine,
            fine,
            jax.ShapeDtypeStruct(FINE_TILED, F32),
            jax.ShapeDtypeStruct((8 * HALF, LANES), F32),
            jax.ShapeDtypeStruct((WIDE, 2 * LANES), BF16),
            jax.ShapeDtypeStruct((2 * LANES, WIDE), BF16),
        ),
        in_specs=[HBM] * 4,
        out_specs=(VMEM,) * 9,
        scratch_shapes=[pltpu.SemaphoreType.DMA((12,))],
        compiler_params=PARAMS,
    )(
        pinned(fine_tiled(velocity)),
        pinned(fine_tiled(forcing)),
        pinned(fine_tiled(viscosity)),
        pinned(coeffs),
    )

    axes = ("grp", "sub")
    count, deep = lax.axis_size(axes), lax.axis_size("sub")

    def swap(block, kept):
        pairs = [(i, i + 1) for i in range(count - 1) if kept(i)]
        return lax.ppermute(block, axes, pairs + [(j, i) for i, j in pairs])

    early_got = swap(early, lambda i: i % 2 == 0 and i % deep < deep - 2)
    half_scratch = [
        pltpu.VMEM((COMPS, 8 * 8, LANES), F32),
        pltpu.VMEM((COMPS,) + FINE_TILED, F32),
    ]
    middle, corrected, upper_fix = pl.pallas_call(
        upper_kernel,
        out_shape=(message, fine, jax.ShapeDtypeStruct((COMPS, 4 * 8, LANES), F32)),
        in_specs=[VMEM, ANY] + [VMEM] * 6,
        out_specs=(ANY, HBM, VMEM),
        input_output_aliases={1: 0},
        scratch_shapes=half_scratch + [pltpu.SemaphoreType.DMA((COMPS, 2))],
        compiler_params=PARAMS,
    )(early, middle, early_got, cross, v_kept, cv_kept, restrict, prolong)
    middle_got = swap(middle, lambda i: i % 2 == 1)
    cross_local = cross
    early, cross = pl.pallas_call(
        late_kernel,
        out_shape=(message, crosses),
        in_specs=[ANY] + [VMEM] * 7,
        out_specs=(VMEM, VMEM),
        compiler_params=PARAMS,
        cost_estimate=pl.CostEstimate(flops=10**9, bytes_accessed=10**7, transcendentals=0),
    )(upper_fix, early, cross, v_kept, f_kept, c_kept, cv_kept, restrict)
    late_got = swap(early, lambda i: i % 2 == 0 and i % deep == deep - 2)

    finish_scratch = half_scratch + [
        pltpu.SemaphoreType.DMA((COMPS, 2)),
        pltpu.VMEM((COMPS, 8 * HALF, LANES), F32),
        pltpu.SemaphoreType.DMA,
    ]
    kept = (v_kept, cv_kept, restrict, prolong)
    corrected, fix = pl.pallas_call(
        lower_kernel,
        out_shape=(fine, coarse),
        in_specs=[HBM] + [VMEM] * 8,
        out_specs=(HBM, HBM),
        input_output_aliases={0: 0},
        scratch_shapes=finish_scratch,
        compiler_params=PARAMS,
    )(pinned(corrected), upper_fix, middle, middle_got, cross_local, *kept)
    corrected, fix = pl.pallas_call(
        finish_kernel,
        out_shape=(fine, coarse),
        in_specs=[HBM, HBM] + [VMEM] * 10,
        out_specs=(HBM, HBM),
        input_output_aliases={0: 0, 1: 1},
        scratch_shapes=finish_scratch,
        compiler_params=PARAMS,
    )(pinned(corrected), pinned(fix), early, middle, middle_got, early_got, late_got, cross, *kept)
    corrected = corrected.reshape(COMPS, 2, TILES, 8, LANES)
    fix = fix.reshape(COMPS, BLOCKS, HALF, LANES)
    return (
        jnp.swapaxes(corrected, 2, 3).reshape(velocity.shape),
        jnp.swapaxes(fix, 1, 2).reshape(COMPS, HALF, COARSE),
    )


def solution(mesh):
    return jax.shard_map(
        shards,
        mesh=mesh,
        in_specs=(
            P(None, ("grp", "sub"), None),
            P(None, ("grp", "sub"), None),
            P(("grp", "sub"), None),
            P(("grp", "sub"), None),
        ),
        out_specs=(P(None, ("grp", "sub"), None), P(None, ("grp", "sub"), None)),
        check_vma=False,
    )
```

```python
import jax
import jax.numpy as jnp
from jax import lax
from jax.experimental import pallas as pl
from jax.experimental.pallas import tpu as pltpu
from jax.sharding import PartitionSpec as P

NY = 32
NZ = 32
DEGREE = 3
LOWER_EIG = 0.15
UPPER_EIG = 1.95
CENTER = 0.5 * (UPPER_EIG + LOWER_EIG)
HALF_WIDTH = 0.5 * (UPPER_EIG - LOWER_EIG)

COMPS = 3
FINE = 4 * NY * NZ
COARSE = NY * NZ
PLANES = 16
HALF = PLANES // 2
LANES = 128
BLOCKS = COARSE // LANES
WIDE = FINE // BLOCKS
TILES = FINE // LANES
F32 = jnp.float32
BF16 = jnp.bfloat16


def tile(index):
    return slice(LANES * index, LANES * (index + 1))


def fill_restrict(ref):
    fine = lax.broadcasted_iota(jnp.int32, (2 * NZ, LANES), 0)
    lane = lax.broadcasted_iota(jnp.int32, (2 * NZ, LANES), 1)
    apart = (fine - 2 * (lane % NZ) + 2 * NZ) % (2 * NZ)
    cols = jnp.where(apart == 0, 1.0, jnp.where((apart == 1) | (apart == 2 * NZ - 1), 0.5, 0.0))
    for row in range(8):
        away = jnp.abs(2 * (lane // NZ) - row)
        rows = jnp.where(away == 0, 1.0, jnp.where(away == 1, 0.5, 0.0))
        at = slice(2 * NZ * row, 2 * NZ * (row + 1))
        ref[at, :LANES] = (cols * rows).astype(BF16)
        beyond = jnp.where(lane < NZ, 0.5 * cols, 0.0) if row == 7 else jnp.zeros_like(cols)
        ref[at, LANES:] = beyond.astype(BF16)


def fill_prolong(ref):
    coarse = lax.broadcasted_iota(jnp.int32, (NZ, LANES), 0)
    lane = lax.broadcasted_iota(jnp.int32, (NZ, LANES), 1)
    apart = (lane - 2 * coarse + 2 * NZ) % (2 * NZ)
    cols = jnp.where(apart == 0, 1.0, jnp.where((apart == 1) | (apart == 2 * NZ - 1), 0.5, 0.0))
    for row in range(8):
        for part in range(4):
            away = jnp.abs(2 * row - 2 * part - lane // (2 * NZ))
            rows = jnp.where(away == 0, 1.0, jnp.where(away == 1, 0.5, 0.0))
            kept = cols * rows if row < 5 else jnp.zeros_like(cols)
            ref[NZ * row : NZ * (row + 1), tile(part)] = kept.astype(BF16)


def split_dot(left, matrix):
    high = left.astype(BF16)
    low = (left - high.astype(F32)).astype(BF16)
    return jnp.dot(high, matrix, preferred_element_type=F32) + jnp.dot(
        low, matrix, preferred_element_type=F32
    )


def iotas(rows):
    row = lax.broadcasted_iota(jnp.int32, (rows, LANES), 0)
    lane = lax.broadcasted_iota(jnp.int32, (rows, LANES), 1)
    return row, lane


def eight(index):
    return slice(8 * index, 8 * (index + 1))


def local_kernel(
    v_hbm,
    f_hbm,
    c_hbm,
    cv_hbm,
    right_ref,
    left_ref,
    cross_ref,
    v_ref,
    cv_ref,
    w_ref,
    q_ref,
    f_vm,
    c_vm,
    sems,
):
    copies = [pltpu.make_async_copy(c_hbm, c_vm, sems.at[0])]
    for k in range(COMPS):
        copies.append(pltpu.make_async_copy(v_hbm.at[k], v_ref.at[k], sems.at[1 + 2 * k]))
        copies.append(pltpu.make_async_copy(f_hbm.at[k], f_vm.at[k], sems.at[2 + 2 * k]))
    copies.append(pltpu.make_async_copy(cv_hbm, cv_ref, sems.at[1 + 2 * COMPS]))
    for copy in copies:
        copy.start()

    row, lane = iotas(PLANES)
    low_half = lane < 64
    first_col = lane % 64 == 0
    last_col = lane % 64 == 63
    fill_restrict(w_ref)
    fill_prolong(q_ref)
    matrix = w_ref[...]

    def packed_planes(slab, source):
        for part in range(4):
            left_ref[slab, :, tile(part)] = source[0, pl.ds(8 * part, 8, 32), :]
            right_ref[slab, :, tile(part)] = source[1, pl.ds(8 * part + 7, 8, 32), :]

    copies[0].wait()
    packed_planes(COMPS, c_vm)

    for k in range(COMPS):
        copies[1 + 2 * k].wait()
        copies[2 + 2 * k].wait()

        def planes_of(ref, t):
            return jnp.concatenate([ref[0, eight(t), :], ref[1, eight(t), :]], axis=0)

        values = [planes_of(v_ref.at[k], t) for t in range(TILES)]
        swapped = [pltpu.roll(x, 64, 1) for x in values]
        blocks = []
        for s in range(BLOCKS):
            pieces = []
            for t in range(4 * s, 4 * s + 4):
                x, turned = values[t], swapped[t]
                beside = turned + jnp.where(low_half, swapped[t - 1], swapped[(t + 1) % TILES])
                beside += pltpu.roll(jnp.where(last_col, turned, x), 1, 1)
                beside += pltpu.roll(jnp.where(first_col, turned, x), LANES - 1, 1)
                beside += jnp.where(row == 0, 0.0, pltpu.roll(x, 1, 0))
                beside += jnp.where(row == PLANES - 1, 0.0, pltpu.roll(x, PLANES - 1, 0))
                pieces.append(
                    planes_of(f_vm.at[k], t) - x + planes_of(c_vm, t) * (beside - 6.0 * x)
                )
            blocks.append(jnp.concatenate(pieces, axis=1))
        sums = split_dot(jnp.concatenate(blocks, axis=0), matrix)
        parts = [sums[PLANES * s : PLANES * (s + 1)] for s in range(BLOCKS)]
        for s in range(BLOCKS):
            crossed = parts[s][:, :LANES] + parts[s - 1][:, LANES:]
            cross_ref[k, PLANES * s : PLANES * (s + 1), :] = crossed
        planes = [cross_ref[k, pl.ds(p, 8, PLANES), :] for p in range(PLANES)]
        half_odds = [0.0625 * planes[2 * j + 1] for j in range(HALF)]
        sources = []
        for j in range(HALF):
            source = 0.125 * planes[2 * j] + half_odds[j]
            if j > 0:
                source += half_odds[j - 1]
            sources.append(source)
        for j in range(3):
            left_ref[4 + j, :, tile(k)] = sources[j]
            right_ref[4 + j, :, tile(k)] = (sources[6:] + half_odds[-1:])[j]
        packed_planes(k, v_ref.at[k])

    copies[-1].wait()
    for j in range(3):
        left_ref[4 + j, :, tile(COMPS)] = cv_ref[pl.ds(j, 8, 8), :]
        right_ref[4 + j, :, tile(COMPS)] = cv_ref[pl.ds(min(6 + j, 7), 8, 8), :]


def finish_half(h, sent, got, cross_ref, v_ref, cv_ref, w_ref, q_ref, mix_vm, out_vm, out_hbm, sems, keep_fix):
    _, lane = iotas(8)
    kept_up = lane < LANES - NZ
    kept_down = lane >= NZ
    first_col = lane % NZ == 0
    last_col = lane % NZ == NZ - 1
    whole = slice(0, WIDE)

    their_coeff, own_coeff = got(COMPS, whole), sent(COMPS, whole)
    rows = [got(k, whole) * own_coeff for k in range(COMPS)]
    rows += [sent(k, whole) * their_coeff for k in range(COMPS)]
    sums = split_dot(jnp.concatenate(rows, axis=0), w_ref[...])
    terms = []
    for part in range(2 * COMPS):
        mine = sums[eight(part)]
        terms.append(mine[:, :LANES] + pltpu.roll(mine[:, LANES:], 1, 0))

    first = 4 * h - 2
    last = first + 8
    inverse, quotient = {}, {}
    for j in range(first, last + 1):
        if j < 0:
            coeff = got(6 + j, tile(COMPS))
        elif j < HALF:
            coeff = cv_ref[pl.ds(j, 8, 8), :]
        else:
            coeff = got(4 + j - HALF, tile(COMPS))
        if j == HALF:
            inside = coeff > 0.0
        inverse[j] = 1.0 / (1.0 + 6.0 * coeff)
        quotient[j] = coeff * inverse[j]

    def near_sum(planes, j):
        x = planes[j]
        up = pltpu.roll(x, LANES - NZ, 1)
        down = pltpu.roll(x, NZ, 1)
        total = planes[j - 1] + planes[j + 1]
        total += jnp.where(kept_up, up, pltpu.roll(up, 7, 0))
        total += jnp.where(kept_down, down, pltpu.roll(down, 1, 0))
        total += pltpu.roll(jnp.where(last_col, up, x), 1, 1)
        total += pltpu.roll(jnp.where(first_col, down, x), LANES - 1, 1)
        return total

    sigma = CENTER / HALF_WIDTH
    stores = []
    for k in range(COMPS):
        at = tile(k)
        theirs, ours = terms[k], terms[COMPS + k]

        def crossed(p):
            return cross_ref[k, pl.ds(p, 8, PLANES), :]

        source = {}
        for j in range(max(first, 0), min(last, HALF - 1) + 1):
            beside = crossed(2 * j + 1)
            if j > 0:
                beside += crossed(2 * j - 1)
            source[j] = 0.125 * crossed(2 * j) + 0.0625 * beside
        if h == 0:
            source[-2] = got(4, at)
            source[-1] = got(5, at) + 0.0625 * ours
            source[0] += got(6, at) + (0.125 * theirs + 0.0625 * ours)
        else:
            source[HALF - 1] += 0.0625 * theirs
            after = sent(6, at) + got(4, at) + (0.0625 * theirs + 0.125 * ours)
            source[HALF] = jnp.where(inside, after, 0.0)
            source[HALF + 1] = got(5, at)
            source[HALF + 2] = got(6, at)

        scaled = {j: source[j] * inverse[j] for j in source}
        update = {j: x * (1.0 / CENTER) for j, x in scaled.items()}
        approx = update
        ratio_old = 1.0 / sigma
        for sweep in range(1, DEGREE):
            ratio_new = 1.0 / (2.0 * sigma - ratio_old)
            keep, gain = ratio_new * ratio_old, 2.0 * ratio_new / HALF_WIDTH
            inner = range(first + sweep, last - sweep + 1)
            update = {
                j: keep * update[j]
                + gain * (scaled[j] - approx[j] + quotient[j] * near_sum(approx, j))
                for j in inner
            }
            approx = {j: approx[j] + update[j] for j in inner}
            ratio_old = ratio_new

        for i in range(4):
            here, after = approx[4 * h + i], approx[4 * h + i + 1]
            keep_fix(k, i, here)
            mix_vm[k, eight(2 * i), :] = here
            mix_vm[k, eight(2 * i + 1), :] = 0.5 * (here + after)
        mixed = [mix_vm[k, pl.ds(s, 8, 8), :] for s in range(BLOCKS)]
        left = [
            jnp.concatenate([mixed[s], mixed[(s + 1) % BLOCKS]], axis=1) for s in range(BLOCKS)
        ]
        fine = split_dot(jnp.concatenate(left, axis=0), q_ref[...])
        for t in range(TILES):
            add = fine[eight(t // 4), tile(t % 4)]
            out_vm[k, h, eight(t), :] = v_ref[k, h, eight(t), :] + add
        store = pltpu.make_async_copy(out_vm.at[k, h], out_hbm.at[k, h], sems.at[k, h])
        store.start()
        stores.append(store)
    return stores


def upper_kernel(
    left_in,
    right_sent,
    inner_got,
    cross_ref,
    v_ref,
    cv_ref,
    w_ref,
    q_ref,
    left_ref,
    out_hbm,
    fix_ref,
    mix_vm,
    out_vm,
    sems,
):
    del left_in, left_ref

    @pl.when(lax.axis_index("sub") == 0)
    def _():
        def keep_fix(k, i, plane):
            fix_ref[k, eight(i), :] = plane

        stores = finish_half(
            1,
            lambda slab, lanes: right_sent[slab, :, lanes],
            lambda slab, lanes: inner_got[slab, :, lanes],
            cross_ref,
            v_ref,
            cv_ref,
            w_ref,
            q_ref,
            mix_vm,
            out_vm,
            out_hbm,
            sems,
            keep_fix,
        )
        for store in stores:
            store.wait()


def lower_kernel(
    out_in,
    upper_fix,
    left_sent,
    right_got,
    cross_ref,
    v_ref,
    cv_ref,
    w_ref,
    q_ref,
    out_hbm,
    fix_hbm,
    mix_vm,
    out_vm,
    sems,
    fix_vm,
    fix_sem,
):
    del out_in

    @pl.when(lax.axis_index("sub") == 0)
    def _():
        def keep_fix(k, i, plane):
            fix_vm[k, pl.ds(i, 8, 8), :] = plane

        for k in range(COMPS):
            for i in range(4):
                fix_vm[k, pl.ds(4 + i, 8, 8), :] = upper_fix[k, eight(i), :]
        stores = finish_half(
            0,
            lambda slab, lanes: left_sent[slab, :, lanes],
            lambda slab, lanes: right_got[slab, :, lanes],
            cross_ref,
            v_ref,
            cv_ref,
            w_ref,
            q_ref,
            mix_vm,
            out_vm,
            out_hbm,
            sems,
            keep_fix,
        )
        fix_copy = pltpu.make_async_copy(fix_vm, fix_hbm, fix_sem)
        fix_copy.start()
        for store in stores:
            store.wait()
        fix_copy.wait()


def finish_kernel(
    out_in,
    fix_in,
    left_sent,
    right_sent,
    right_got,
    inner_got,
    outer_got,
    cross_ref,
    v_ref,
    cv_ref,
    w_ref,
    q_ref,
    out_hbm,
    fix_hbm,
    mix_vm,
    out_vm,
    sems,
    fix_vm,
    fix_sem,
):
    del out_in, fix_in
    at = lax.axis_index("sub")
    inner = at < lax.axis_size("sub") - 2

    def left_got(slab, lanes):
        return jnp.where(inner, inner_got[slab, :, lanes], outer_got[slab, :, lanes])

    def half(which, sent, got):
        def keep_fix(k, i, plane):
            fix_vm[k, pl.ds(4 * which + i, 8, 8), :] = plane

        refs = (cross_ref, v_ref, cv_ref, w_ref, q_ref, mix_vm, out_vm, out_hbm, sems, keep_fix)
        return finish_half(which, lambda slab, lanes: sent[slab, :, lanes], got, *refs)

    @pl.when(at != 0)
    def _():
        stores = half(0, left_sent, lambda slab, lanes: right_got[slab, :, lanes])
        stores += half(1, right_sent, left_got)
        fix_copy = pltpu.make_async_copy(fix_vm, fix_hbm, fix_sem)
        fix_copy.start()
        for store in stores:
            store.wait()
        fix_copy.wait()


VMEM = pl.BlockSpec(memory_space=pltpu.VMEM)
HBM = pl.BlockSpec(memory_space=pltpu.HBM)
ANY = pl.BlockSpec(memory_space=pl.ANY)
PARAMS = pltpu.CompilerParams(vmem_limit_bytes=16 * 2**20)
FINE_TILED = (2, 8 * TILES, LANES)


def fine_tiled(field):
    lead = field.shape[:-2]
    split = field.reshape(lead + (2, 8, TILES, LANES))
    return jnp.swapaxes(split, -3, -2).reshape(lead + FINE_TILED)


def pinned(field):
    return pltpu.with_memory_space_constraint(field, pltpu.HBM)


def shards(velocity, forcing, viscosity, coarse_visc):
    coeffs = jnp.swapaxes(coarse_visc.reshape(HALF, BLOCKS, LANES), 0, 1).reshape(8 * HALF, LANES)
    message = jax.ShapeDtypeStruct((7, 8, WIDE), F32)
    fine = jax.ShapeDtypeStruct((COMPS,) + FINE_TILED, F32)
    coarse = jax.ShapeDtypeStruct((COMPS, 8 * HALF, LANES), F32)
    crosses = jax.ShapeDtypeStruct((COMPS, 8 * PLANES, LANES), F32)
    right_sent, left_sent, cross, *kept = pl.pallas_call(
        local_kernel,
        out_shape=(
            message,
            message,
            crosses,
            fine,
            jax.ShapeDtypeStruct((8 * HALF, LANES), F32),
            jax.ShapeDtypeStruct((WIDE, 2 * LANES), BF16),
            jax.ShapeDtypeStruct((2 * LANES, WIDE), BF16),
        ),
        in_specs=[HBM] * 4,
        out_specs=(VMEM,) * 7,
        scratch_shapes=[
            pltpu.VMEM((COMPS,) + FINE_TILED, F32),
            pltpu.VMEM(FINE_TILED, F32),
            pltpu.SemaphoreType.DMA((2 + 2 * COMPS,)),
        ],
        compiler_params=PARAMS,
    )(
        pinned(fine_tiled(velocity)),
        pinned(fine_tiled(forcing)),
        pinned(fine_tiled(viscosity)),
        pinned(coeffs),
    )

    axes = ("grp", "sub")
    count, deep = lax.axis_size(axes), lax.axis_size("sub")
    inner = [(i + 1, i) for i in range(count - 1) if i % deep < deep - 2]
    outer = [(i + 1, i) for i in range(count - 1) if i % deep >= deep - 2]
    right_got = lax.ppermute(right_sent, axes, [(i, i + 1) for i in range(count - 1)])
    inner_got = lax.ppermute(left_sent, axes, inner)
    half_scratch = [
        pltpu.VMEM((COMPS, 8 * 8, LANES), F32),
        pltpu.VMEM((COMPS,) + FINE_TILED, F32),
    ]
    left_sent, corrected, upper_fix = pl.pallas_call(
        upper_kernel,
        out_shape=(message, fine, jax.ShapeDtypeStruct((COMPS, 4 * 8, LANES), F32)),
        in_specs=[ANY] + [VMEM] * 7,
        out_specs=(ANY, HBM, VMEM),
        input_output_aliases={0: 0},
        scratch_shapes=half_scratch + [pltpu.SemaphoreType.DMA((COMPS, 2))],
        compiler_params=PARAMS,
    )(left_sent, right_sent, inner_got, cross, *kept)
    outer_got = lax.ppermute(left_sent, axes, outer)
    finish_scratch = half_scratch + [
        pltpu.SemaphoreType.DMA((COMPS, 2)),
        pltpu.VMEM((COMPS, 8 * HALF, LANES), F32),
        pltpu.SemaphoreType.DMA,
    ]
    corrected, fix = pl.pallas_call(
        lower_kernel,
        out_shape=(fine, coarse),
        in_specs=[HBM] + [VMEM] * 8,
        out_specs=(HBM, HBM),
        input_output_aliases={0: 0},
        scratch_shapes=finish_scratch,
        compiler_params=PARAMS,
    )(pinned(corrected), upper_fix, left_sent, right_got, cross, *kept)
    corrected, fix = pl.pallas_call(
        finish_kernel,
        out_shape=(fine, coarse),
        in_specs=[HBM, HBM] + [VMEM] * 10,
        out_specs=(HBM, HBM),
        input_output_aliases={0: 0, 1: 1},
        scratch_shapes=finish_scratch,
        compiler_params=PARAMS,
    )(
        pinned(corrected),
        pinned(fix),
        left_sent,
        right_sent,
        right_got,
        inner_got,
        outer_got,
        cross,
        *kept,
    )
    corrected = corrected.reshape(COMPS, 2, TILES, 8, LANES)
    fix = fix.reshape(COMPS, BLOCKS, HALF, LANES)
    return (
        jnp.swapaxes(corrected, 2, 3).reshape(velocity.shape),
        jnp.swapaxes(fix, 1, 2).reshape(COMPS, HALF, COARSE),
    )


def solution(mesh):
    return jax.shard_map(
        shards,
        mesh=mesh,
        in_specs=(
            P(None, ("grp", "sub"), None),
            P(None, ("grp", "sub"), None),
            P(("grp", "sub"), None),
            P(("grp", "sub"), None),
        ),
        out_specs=(P(None, ("grp", "sub"), None), P(None, ("grp", "sub"), None)),
        check_vma=False,
    )
```

```python
import jax
import jax.numpy as jnp
from jax import lax
from jax.experimental import pallas as pl
from jax.experimental.pallas import tpu as pltpu
from jax.sharding import PartitionSpec as P

NY = 32
NZ = 32
DEGREE = 3
LOWER_EIG = 0.15
UPPER_EIG = 1.95
CENTER = 0.5 * (UPPER_EIG + LOWER_EIG)
HALF_WIDTH = 0.5 * (UPPER_EIG - LOWER_EIG)

COMPS = 3
FINE = 4 * NY * NZ
COARSE = NY * NZ
PLANES = 16
HALF = PLANES // 2
LANES = 128
BLOCKS = COARSE // LANES
WIDE = FINE // BLOCKS
TILES = FINE // LANES
F32 = jnp.float32
BF16 = jnp.bfloat16


def tile(index):
    return slice(LANES * index, LANES * (index + 1))


def fill_restrict(ref):
    fine = lax.broadcasted_iota(jnp.int32, (2 * NZ, LANES), 0)
    lane = lax.broadcasted_iota(jnp.int32, (2 * NZ, LANES), 1)
    apart = (fine - 2 * (lane % NZ) + 2 * NZ) % (2 * NZ)
    cols = jnp.where(apart == 0, 1.0, jnp.where((apart == 1) | (apart == 2 * NZ - 1), 0.5, 0.0))
    for row in range(8):
        away = jnp.abs(2 * (lane // NZ) - row)
        rows = jnp.where(away == 0, 1.0, jnp.where(away == 1, 0.5, 0.0))
        at = slice(2 * NZ * row, 2 * NZ * (row + 1))
        ref[at, :LANES] = (cols * rows).astype(BF16)
        beyond = jnp.where(lane < NZ, 0.5 * cols, 0.0) if row == 7 else jnp.zeros_like(cols)
        ref[at, LANES:] = beyond.astype(BF16)


def fill_prolong(ref):
    coarse = lax.broadcasted_iota(jnp.int32, (NZ, LANES), 0)
    lane = lax.broadcasted_iota(jnp.int32, (NZ, LANES), 1)
    apart = (lane - 2 * coarse + 2 * NZ) % (2 * NZ)
    cols = jnp.where(apart == 0, 1.0, jnp.where((apart == 1) | (apart == 2 * NZ - 1), 0.5, 0.0))
    for row in range(8):
        for part in range(4):
            away = jnp.abs(2 * row - 2 * part - lane // (2 * NZ))
            rows = jnp.where(away == 0, 1.0, jnp.where(away == 1, 0.5, 0.0))
            kept = cols * rows if row < 5 else jnp.zeros_like(cols)
            ref[NZ * row : NZ * (row + 1), tile(part)] = kept.astype(BF16)


def split_dot(left, matrix):
    high = left.astype(BF16)
    low = (left - high.astype(F32)).astype(BF16)
    return jnp.dot(high, matrix, preferred_element_type=F32) + jnp.dot(
        low, matrix, preferred_element_type=F32
    )


def iotas(rows):
    row = lax.broadcasted_iota(jnp.int32, (rows, LANES), 0)
    lane = lax.broadcasted_iota(jnp.int32, (rows, LANES), 1)
    return row, lane


def eight(index):
    return slice(8 * index, 8 * (index + 1))


def local_kernel(
    v_hbm,
    f_hbm,
    c_hbm,
    cv_hbm,
    near_ref,
    far_ref,
    src_ref,
    v_ref,
    cv_ref,
    w_ref,
    q_ref,
    f_vm,
    c_vm,
    cross_vm,
    sems,
):
    copies = [pltpu.make_async_copy(c_hbm, c_vm, sems.at[0])]
    for k in range(COMPS):
        copies.append(pltpu.make_async_copy(v_hbm.at[k], v_ref.at[k], sems.at[1 + 2 * k]))
        copies.append(pltpu.make_async_copy(f_hbm.at[k], f_vm.at[k], sems.at[2 + 2 * k]))
    copies.append(pltpu.make_async_copy(cv_hbm, cv_ref, sems.at[1 + 2 * COMPS]))
    for copy in copies:
        copy.start()

    even = lax.rem(lax.axis_index("sub"), 2) == 0
    row, lane = iotas(PLANES)
    low_half = lane < 64
    first_col = lane % 64 == 0
    last_col = lane % 64 == 63
    fill_restrict(w_ref)
    fill_prolong(q_ref)
    matrix = w_ref[...]

    def send(slab, lanes, to_left, to_right):
        near_ref[slab, :, lanes] = jnp.where(even, to_right, to_left)
        far_ref[slab, :, lanes] = jnp.where(even, to_left, to_right)

    def packed_planes(slab, source):
        for part in range(4):
            first = source[0, pl.ds(8 * part, 8, 32), :]
            send(slab, tile(part), first, source[1, pl.ds(8 * part + 7, 8, 32), :])

    copies[0].wait()
    packed_planes(COMPS, c_vm)

    for k in range(COMPS):
        copies[1 + 2 * k].wait()
        copies[2 + 2 * k].wait()

        def planes_of(ref, t):
            return jnp.concatenate([ref[0, eight(t), :], ref[1, eight(t), :]], axis=0)

        values = [planes_of(v_ref.at[k], t) for t in range(TILES)]
        swapped = [pltpu.roll(x, 64, 1) for x in values]
        blocks = []
        for s in range(BLOCKS):
            pieces = []
            for t in range(4 * s, 4 * s + 4):
                x, turned = values[t], swapped[t]
                beside = turned + jnp.where(low_half, swapped[t - 1], swapped[(t + 1) % TILES])
                beside += pltpu.roll(jnp.where(last_col, turned, x), 1, 1)
                beside += pltpu.roll(jnp.where(first_col, turned, x), LANES - 1, 1)
                beside += jnp.where(row == 0, 0.0, pltpu.roll(x, 1, 0))
                beside += jnp.where(row == PLANES - 1, 0.0, pltpu.roll(x, PLANES - 1, 0))
                pieces.append(
                    planes_of(f_vm.at[k], t) - x + planes_of(c_vm, t) * (beside - 6.0 * x)
                )
            blocks.append(jnp.concatenate(pieces, axis=1))
        sums = split_dot(jnp.concatenate(blocks, axis=0), matrix)
        parts = [sums[PLANES * s : PLANES * (s + 1)] for s in range(BLOCKS)]
        for s in range(BLOCKS):
            crossed = parts[s][:, :LANES] + parts[s - 1][:, LANES:]
            cross_vm[k, PLANES * s : PLANES * (s + 1), :] = crossed
        planes = [cross_vm[k, pl.ds(p, 8, PLANES), :] for p in range(PLANES)]
        half_odds = [0.0625 * planes[2 * j + 1] for j in range(HALF)]
        sources = []
        for j in range(HALF):
            source = 0.125 * planes[2 * j] + half_odds[j]
            if j > 0:
                source += half_odds[j - 1]
            src_ref[k, eight(j), :] = source
            sources.append(source)
        for j in range(3):
            send(4 + j, tile(k), sources[j], (sources[6:] + half_odds[-1:])[j])
        packed_planes(k, v_ref.at[k])

    copies[-1].wait()
    for j in range(3):
        first = cv_ref[pl.ds(j, 8, 8), :]
        send(4 + j, tile(COMPS), first, cv_ref[pl.ds(min(6 + j, 7), 8, 8), :])


def finish_kernel(
    v_ref,
    cv_ref,
    src_ref,
    near_sent,
    far_sent,
    near_hbm,
    far_hbm,
    w_ref,
    q_ref,
    out_hbm,
    fix_hbm,
    near_got,
    far_got,
    got_sems,
    out_vm,
    mix_vm,
    sems,
    fix_ref,
    fix_sem,
):
    at_sub, at_grp = lax.axis_index("sub"), lax.axis_index("grp")
    odd = lax.rem(at_sub, 2)
    even = odd == 0
    fetches = [
        pltpu.make_async_copy(far_hbm.at[odd], far_got, got_sems.at[0]),
        pltpu.make_async_copy(near_hbm.at[1 - odd], near_got, got_sems.at[1]),
    ]
    for fetch in fetches:
        fetch.start()
    for fetch in fetches:
        fetch.wait()
    begin = (at_sub == 0) & (at_grp == 0)
    end = (at_sub == lax.axis_size("sub") - 1) & (at_grp == lax.axis_size("grp") - 1)

    def left_sent(slab, lanes):
        return jnp.where(even, far_sent[slab, :, lanes], near_sent[slab, :, lanes])

    def right_sent(slab, lanes):
        return jnp.where(even, near_sent[slab, :, lanes], far_sent[slab, :, lanes])

    def right_got(slab, lanes):
        value = jnp.where(even, far_got[slab, :, lanes], near_got[slab, :, lanes])
        return jnp.where(begin, 0.0, value)

    def left_got(slab, lanes):
        value = jnp.where(even, near_got[slab, :, lanes], far_got[slab, :, lanes])
        return jnp.where(end, 0.0, value)

    whole = slice(0, WIDE)
    _, lane = iotas(8)
    kept_up = lane < LANES - NZ
    kept_down = lane >= NZ
    first_col = lane % NZ == 0
    last_col = lane % NZ == NZ - 1

    rows = []
    for sent, got in ((left_sent, right_got), (right_sent, left_got)):
        own_coeff, their_coeff = sent(COMPS, whole), got(COMPS, whole)
        rows += [got(k, whole) * own_coeff for k in range(COMPS)]
        rows += [sent(k, whole) * their_coeff for k in range(COMPS)]
    sums = split_dot(jnp.concatenate(rows, axis=0), w_ref[...])
    terms = []
    for part in range(len(rows)):
        mine = sums[eight(part)]
        terms.append(mine[:, :LANES] + pltpu.roll(mine[:, LANES:], 1, 0))

    first, last = -2, HALF + 2
    inverse, quotient = {}, {}
    for j in range(first, last + 1):
        if j < 0:
            coeff = right_got(6 + j, tile(COMPS))
        elif j < HALF:
            coeff = cv_ref[pl.ds(j, 8, 8), :]
        else:
            coeff = left_got(4 + j - HALF, tile(COMPS))
        if j == HALF:
            inside = coeff > 0.0
        inverse[j] = 1.0 / (1.0 + 6.0 * coeff)
        quotient[j] = coeff * inverse[j]

    def near_sum(planes, j):
        x = planes[j]
        up = pltpu.roll(x, LANES - NZ, 1)
        down = pltpu.roll(x, NZ, 1)
        total = planes[j - 1] + planes[j + 1]
        total += jnp.where(kept_up, up, pltpu.roll(up, 7, 0))
        total += jnp.where(kept_down, down, pltpu.roll(down, 1, 0))
        total += pltpu.roll(jnp.where(last_col, up, x), 1, 1)
        total += pltpu.roll(jnp.where(first_col, down, x), LANES - 1, 1)
        return total

    sigma = CENTER / HALF_WIDTH
    stores = []
    for k in range(COMPS):
        at = tile(k)
        left_theirs, left_ours = terms[k], terms[COMPS + k]
        right_theirs, right_ours = terms[2 * COMPS + k], terms[3 * COMPS + k]
        source = {j: src_ref[k, eight(j), :] for j in range(HALF)}
        source[-2] = right_got(4, at)
        source[-1] = right_got(5, at) + 0.0625 * left_ours
        source[0] += right_got(6, at) + (0.125 * left_theirs + 0.0625 * left_ours)
        source[HALF - 1] += 0.0625 * right_theirs
        after = right_sent(6, at) + left_got(4, at) + (0.0625 * right_theirs + 0.125 * right_ours)
        source[HALF] = jnp.where(inside, after, 0.0)
        source[HALF + 1] = left_got(5, at)
        source[HALF + 2] = left_got(6, at)

        scaled = {j: source[j] * inverse[j] for j in source}
        update = {j: x * (1.0 / CENTER) for j, x in scaled.items()}
        approx = update
        ratio_old = 1.0 / sigma
        for sweep in range(1, DEGREE):
            ratio_new = 1.0 / (2.0 * sigma - ratio_old)
            keep, gain = ratio_new * ratio_old, 2.0 * ratio_new / HALF_WIDTH
            inner = range(first + sweep, last - sweep + 1)
            update = {
                j: keep * update[j]
                + gain * (scaled[j] - approx[j] + quotient[j] * near_sum(approx, j))
                for j in inner
            }
            approx = {j: approx[j] + update[j] for j in inner}
            ratio_old = ratio_new

        for j in range(HALF):
            fix_ref[k, pl.ds(j, 8, 8), :] = approx[j]
            mix_vm[k, eight(2 * j), :] = approx[j]
            mix_vm[k, eight(2 * j + 1), :] = 0.5 * (approx[j] + approx[j + 1])
        mixed = [
            [mix_vm[k, pl.ds(64 * h + s, 8, 8), :] for s in range(BLOCKS)] for h in range(2)
        ]
        left = [
            jnp.concatenate([mixed[h][s], mixed[h][(s + 1) % BLOCKS]], axis=1)
            for h in range(2)
            for s in range(BLOCKS)
        ]
        fine = split_dot(jnp.concatenate(left, axis=0), q_ref[...])
        for h in range(2):
            for t in range(TILES):
                add = fine[eight(BLOCKS * h + t // 4), tile(t % 4)]
                out_vm[k, h, eight(t), :] = v_ref[k, h, eight(t), :] + add
        store = pltpu.make_async_copy(out_vm.at[k], out_hbm.at[k], sems.at[k])
        store.start()
        stores.append(store)
    stores.append(pltpu.make_async_copy(fix_ref, fix_hbm, fix_sem))
    stores[-1].start()
    for store in stores:
        store.wait()


VMEM = pl.BlockSpec(memory_space=pltpu.VMEM)
HBM = pl.BlockSpec(memory_space=pltpu.HBM)
LIMIT = 16 * 2**20
FINE_TILED = (2, 8 * TILES, LANES)


def fine_tiled(field):
    lead = field.shape[:-2]
    split = field.reshape(lead + (2, 8, TILES, LANES))
    return jnp.swapaxes(split, -3, -2).reshape(lead + FINE_TILED)


def pinned(field):
    return pltpu.with_memory_space_constraint(fine_tiled(field), pltpu.HBM)


def pinned_as_is(field):
    return pltpu.with_memory_space_constraint(field, pltpu.HBM)


def shards(velocity, forcing, viscosity, coarse_visc):
    coeffs = jnp.swapaxes(coarse_visc.reshape(HALF, BLOCKS, LANES), 0, 1).reshape(8 * HALF, LANES)
    coeffs = pltpu.with_memory_space_constraint(coeffs, pltpu.HBM)
    message = jax.ShapeDtypeStruct((7, 8, WIDE), F32)
    fine = jax.ShapeDtypeStruct((COMPS,) + FINE_TILED, F32)
    coarse = jax.ShapeDtypeStruct((COMPS, 8 * HALF, LANES), F32)
    near_sent, far_sent, source, kept, coeffs, restrict, prolong = pl.pallas_call(
        local_kernel,
        out_shape=(
            message,
            message,
            coarse,
            fine,
            jax.ShapeDtypeStruct((8 * HALF, LANES), F32),
            jax.ShapeDtypeStruct((WIDE, 2 * LANES), BF16),
            jax.ShapeDtypeStruct((2 * LANES, WIDE), BF16),
        ),
        in_specs=[HBM] * 4,
        out_specs=(VMEM,) * 7,
        scratch_shapes=[
            pltpu.VMEM((COMPS,) + FINE_TILED, F32),
            pltpu.VMEM(FINE_TILED, F32),
            pltpu.VMEM((COMPS, 8 * PLANES, LANES), F32),
            pltpu.SemaphoreType.DMA((2 + 2 * COMPS,)),
        ],
        compiler_params=pltpu.CompilerParams(vmem_limit_bytes=LIMIT),
    )(pinned(velocity), pinned(forcing), pinned(viscosity), coeffs)

    axes = ("grp", "sub")
    count = lax.axis_size(axes)
    near = [[i, i + 1] for i in range(0, count, 2)]
    far = [[i, (i + 1) % count] for i in range(1, count, 2)]
    far_got = lax.all_gather(far_sent, axes, axis_index_groups=far)
    near_got = lax.all_gather(near_sent, axes, axis_index_groups=near)

    corrected, fix = pl.pallas_call(
        finish_kernel,
        out_shape=(fine, coarse),
        in_specs=[VMEM] * 5 + [HBM] * 2 + [VMEM] * 2,
        out_specs=(HBM, HBM),
        scratch_shapes=[
            pltpu.VMEM(message.shape, F32),
            pltpu.VMEM(message.shape, F32),
            pltpu.SemaphoreType.DMA((2,)),
            pltpu.VMEM((COMPS,) + FINE_TILED, F32),
            pltpu.VMEM((COMPS, 8 * PLANES, LANES), F32),
            pltpu.SemaphoreType.DMA((COMPS,)),
            pltpu.VMEM((COMPS, 8 * HALF, LANES), F32),
            pltpu.SemaphoreType.DMA,
        ],
        compiler_params=pltpu.CompilerParams(vmem_limit_bytes=LIMIT),
    )(kept, coeffs, source, near_sent, far_sent, pinned_as_is(near_got), pinned_as_is(far_got), restrict, prolong)
    corrected = corrected.reshape(COMPS, 2, TILES, 8, LANES)
    fix = fix.reshape(COMPS, BLOCKS, HALF, LANES)
    return (
        jnp.swapaxes(corrected, 2, 3).reshape(velocity.shape),
        jnp.swapaxes(fix, 1, 2).reshape(COMPS, HALF, COARSE),
    )


def solution(mesh):
    return jax.shard_map(
        shards,
        mesh=mesh,
        in_specs=(
            P(None, ("grp", "sub"), None),
            P(None, ("grp", "sub"), None),
            P(("grp", "sub"), None),
            P(("grp", "sub"), None),
        ),
        out_specs=(P(None, ("grp", "sub"), None), P(None, ("grp", "sub"), None)),
        check_vma=False,
    )
```

```python
import jax
import jax.numpy as jnp
from jax import lax
from jax.experimental import pallas as pl
from jax.experimental.pallas import tpu as pltpu
from jax.sharding import PartitionSpec as P

NY = 32
NZ = 32
DEGREE = 3
LOWER_EIG = 0.15
UPPER_EIG = 1.95
CENTER = 0.5 * (UPPER_EIG + LOWER_EIG)
HALF_WIDTH = 0.5 * (UPPER_EIG - LOWER_EIG)

COMPS = 3
FINE = 4 * NY * NZ
COARSE = NY * NZ
PLANES = 16
HALF = PLANES // 2
LANES = 128
BLOCKS = COARSE // LANES
WIDE = FINE // BLOCKS
TILES = FINE // LANES
F32 = jnp.float32
BF16 = jnp.bfloat16


def tile(index):
    return slice(LANES * index, LANES * (index + 1))


def fill_restrict(ref):
    fine = lax.broadcasted_iota(jnp.int32, (2 * NZ, LANES), 0)
    lane = lax.broadcasted_iota(jnp.int32, (2 * NZ, LANES), 1)
    apart = (fine - 2 * (lane % NZ) + 2 * NZ) % (2 * NZ)
    cols = jnp.where(apart == 0, 1.0, jnp.where((apart == 1) | (apart == 2 * NZ - 1), 0.5, 0.0))
    for row in range(8):
        away = jnp.abs(2 * (lane // NZ) - row)
        rows = jnp.where(away == 0, 1.0, jnp.where(away == 1, 0.5, 0.0))
        at = slice(2 * NZ * row, 2 * NZ * (row + 1))
        ref[at, :LANES] = (cols * rows).astype(BF16)
        beyond = jnp.where(lane < NZ, 0.5 * cols, 0.0) if row == 7 else jnp.zeros_like(cols)
        ref[at, LANES:] = beyond.astype(BF16)


def fill_prolong(ref):
    coarse = lax.broadcasted_iota(jnp.int32, (NZ, LANES), 0)
    lane = lax.broadcasted_iota(jnp.int32, (NZ, LANES), 1)
    apart = (lane - 2 * coarse + 2 * NZ) % (2 * NZ)
    cols = jnp.where(apart == 0, 1.0, jnp.where((apart == 1) | (apart == 2 * NZ - 1), 0.5, 0.0))
    for row in range(8):
        for part in range(4):
            away = jnp.abs(2 * row - 2 * part - lane // (2 * NZ))
            rows = jnp.where(away == 0, 1.0, jnp.where(away == 1, 0.5, 0.0))
            kept = cols * rows if row < 5 else jnp.zeros_like(cols)
            ref[NZ * row : NZ * (row + 1), tile(part)] = kept.astype(BF16)


def halves(values):
    high = values.astype(BF16)
    return high, (values - high.astype(F32)).astype(BF16)


def split_dot(left, matrix):
    rows = left.shape[0]
    sums = jnp.dot(jnp.concatenate(halves(left), axis=0), matrix, preferred_element_type=F32)
    return sums[:rows] + sums[rows:]


def iotas(rows):
    row = lax.broadcasted_iota(jnp.int32, (rows, LANES), 0)
    lane = lax.broadcasted_iota(jnp.int32, (rows, LANES), 1)
    return row, lane


def eight(index):
    return slice(8 * index, 8 * (index + 1))


def local_kernel(
    v_hbm,
    f_hbm,
    c_hbm,
    cv_hbm,
    right_ref,
    left_ref,
    cross_ref,
    v_ref,
    cv_ref,
    w_ref,
    q_ref,
    f_vm,
    c_vm,
    split_vm,
    sems,
):
    copies = [pltpu.make_async_copy(c_hbm, c_vm, sems.at[0])]
    for k in range(COMPS):
        copies.append(pltpu.make_async_copy(v_hbm.at[k], v_ref.at[k], sems.at[1 + 2 * k]))
        copies.append(pltpu.make_async_copy(f_hbm.at[k], f_vm.at[k], sems.at[2 + 2 * k]))
    copies.append(pltpu.make_async_copy(cv_hbm, cv_ref, sems.at[1 + 2 * COMPS]))
    for copy in copies:
        copy.start()

    row, lane = iotas(PLANES)
    low_half = lane < 64
    first_col = lane % 64 == 0
    last_col = lane % 64 == 63
    fill_restrict(w_ref)
    fill_prolong(q_ref)

    def packed_planes(slab, source):
        for part in range(4):
            left_ref[slab, :, tile(part)] = source[0, pl.ds(8 * part, 8, 32), :]
            right_ref[slab, :, tile(part)] = source[1, pl.ds(8 * part + 7, 8, 32), :]

    copies[0].wait()
    packed_planes(COMPS, c_vm)

    for k in range(COMPS):
        copies[1 + 2 * k].wait()
        copies[2 + 2 * k].wait()

        def planes_of(ref, t):
            return jnp.concatenate([ref[0, eight(t), :], ref[1, eight(t), :]], axis=0)

        values = [planes_of(v_ref.at[k], t) for t in range(TILES)]
        swapped = [pltpu.roll(x, 64, 1) for x in values]
        for s in range(BLOCKS):
            at = slice(PLANES * (BLOCKS * k + s), PLANES * (BLOCKS * k + s + 1))
            for t in range(4 * s, 4 * s + 4):
                x, turned = values[t], swapped[t]
                beside = turned + jnp.where(low_half, swapped[t - 1], swapped[(t + 1) % TILES])
                beside += pltpu.roll(jnp.where(last_col, turned, x), 1, 1)
                beside += pltpu.roll(jnp.where(first_col, turned, x), LANES - 1, 1)
                beside += jnp.where(row == 0, 0.0, pltpu.roll(x, 1, 0))
                beside += jnp.where(row == PLANES - 1, 0.0, pltpu.roll(x, PLANES - 1, 0))
                residual = planes_of(f_vm.at[k], t) - x + planes_of(c_vm, t) * (beside - 6.0 * x)
                for part, value in enumerate(halves(residual)):
                    split_vm[part, at, tile(t % 4)] = value

    matrix = w_ref[...]
    sums = jnp.dot(split_vm[0], matrix, preferred_element_type=F32)
    sums += jnp.dot(split_vm[1], matrix, preferred_element_type=F32)
    for k in range(COMPS):
        mine = sums[PLANES * BLOCKS * k : PLANES * BLOCKS * (k + 1)]
        parts = [mine[PLANES * s : PLANES * (s + 1)] for s in range(BLOCKS)]
        for s in range(BLOCKS):
            crossed = parts[s][:, :LANES] + parts[s - 1][:, LANES:]
            cross_ref[k, PLANES * s : PLANES * (s + 1), :] = crossed
    for k in range(COMPS):
        planes = [cross_ref[k, pl.ds(p, 8, PLANES), :] for p in range(PLANES)]
        half_odds = [0.0625 * planes[2 * j + 1] for j in range(HALF)]
        sources = []
        for j in range(HALF):
            source = 0.125 * planes[2 * j] + half_odds[j]
            if j > 0:
                source += half_odds[j - 1]
            sources.append(source)
        for j in range(3):
            left_ref[4 + j, :, tile(k)] = sources[j]
            right_ref[4 + j, :, tile(k)] = (sources[6:] + half_odds[-1:])[j]
        packed_planes(k, v_ref.at[k])

    copies[-1].wait()
    for j in range(3):
        left_ref[4 + j, :, tile(COMPS)] = cv_ref[pl.ds(j, 8, 8), :]
        right_ref[4 + j, :, tile(COMPS)] = cv_ref[pl.ds(min(6 + j, 7), 8, 8), :]


def finish_half(h, sent, got, cross_ref, v_ref, cv_ref, w_ref, q_ref, mix_vm, out_vm, out_hbm, sems, keep_fix):
    _, lane = iotas(8)
    kept_up = lane < LANES - NZ
    kept_down = lane >= NZ
    first_col = lane % NZ == 0
    last_col = lane % NZ == NZ - 1
    whole = slice(0, WIDE)

    their_coeff, own_coeff = got(COMPS, whole), sent(COMPS, whole)
    rows = [got(k, whole) * own_coeff for k in range(COMPS)]
    rows += [sent(k, whole) * their_coeff for k in range(COMPS)]
    sums = split_dot(jnp.concatenate(rows, axis=0), w_ref[...])
    terms = []
    for part in range(2 * COMPS):
        mine = sums[eight(part)]
        terms.append(mine[:, :LANES] + pltpu.roll(mine[:, LANES:], 1, 0))

    first = 4 * h - 2
    last = first + 8
    inverse, quotient = {}, {}
    for j in range(first, last + 1):
        if j < 0:
            coeff = got(6 + j, tile(COMPS))
        elif j < HALF:
            coeff = cv_ref[pl.ds(j, 8, 8), :]
        else:
            coeff = got(4 + j - HALF, tile(COMPS))
        if j == HALF:
            inside = coeff > 0.0
        inverse[j] = 1.0 / (1.0 + 6.0 * coeff)
        quotient[j] = coeff * inverse[j]

    def near_sum(planes, j):
        x = planes[j]
        up = pltpu.roll(x, LANES - NZ, 1)
        down = pltpu.roll(x, NZ, 1)
        total = planes[j - 1] + planes[j + 1]
        total += jnp.where(kept_up, up, pltpu.roll(up, 7, 0))
        total += jnp.where(kept_down, down, pltpu.roll(down, 1, 0))
        total += pltpu.roll(jnp.where(last_col, up, x), 1, 1)
        total += pltpu.roll(jnp.where(first_col, down, x), LANES - 1, 1)
        return total

    sigma = CENTER / HALF_WIDTH
    for k in range(COMPS):
        at = tile(k)
        theirs, ours = terms[k], terms[COMPS + k]

        def crossed(p):
            return cross_ref[k, pl.ds(p, 8, PLANES), :]

        source = {}
        for j in range(max(first, 0), min(last, HALF - 1) + 1):
            beside = crossed(2 * j + 1)
            if j > 0:
                beside += crossed(2 * j - 1)
            source[j] = 0.125 * crossed(2 * j) + 0.0625 * beside
        if h == 0:
            source[-2] = got(4, at)
            source[-1] = got(5, at) + 0.0625 * ours
            source[0] += got(6, at) + (0.125 * theirs + 0.0625 * ours)
        else:
            source[HALF - 1] += 0.0625 * theirs
            after = sent(6, at) + got(4, at) + (0.0625 * theirs + 0.125 * ours)
            source[HALF] = jnp.where(inside, after, 0.0)
            source[HALF + 1] = got(5, at)
            source[HALF + 2] = got(6, at)

        scaled = {j: source[j] * inverse[j] for j in source}
        update = {j: x * (1.0 / CENTER) for j, x in scaled.items()}
        approx = update
        ratio_old = 1.0 / sigma
        for sweep in range(1, DEGREE):
            ratio_new = 1.0 / (2.0 * sigma - ratio_old)
            keep, gain = ratio_new * ratio_old, 2.0 * ratio_new / HALF_WIDTH
            inner = range(first + sweep, last - sweep + 1)
            update = {
                j: keep * update[j]
                + gain * (scaled[j] - approx[j] + quotient[j] * near_sum(approx, j))
                for j in inner
            }
            approx = {j: approx[j] + update[j] for j in inner}
            ratio_old = ratio_new

        for i in range(4):
            here, after = approx[4 * h + i], approx[4 * h + i + 1]
            keep_fix(k, i, here)
            mix_vm[k, eight(2 * i), :] = here
            mix_vm[k, eight(2 * i + 1), :] = 0.5 * (here + after)
    left = []
    for k in range(COMPS):
        mixed = [mix_vm[k, pl.ds(s, 8, 8), :] for s in range(BLOCKS)]
        left += [
            jnp.concatenate([mixed[s], mixed[(s + 1) % BLOCKS]], axis=1) for s in range(BLOCKS)
        ]
    fine = split_dot(jnp.concatenate(left, axis=0), q_ref[...])
    stores = []
    for k in range(COMPS):
        for t in range(TILES):
            add = fine[eight(BLOCKS * k + t // 4), tile(t % 4)]
            out_vm[k, h, eight(t), :] = v_ref[k, h, eight(t), :] + add
        store = pltpu.make_async_copy(out_vm.at[k, h], out_hbm.at[k, h], sems.at[k, h])
        store.start()
        stores.append(store)
    return stores


def upper_kernel(
    left_in,
    right_sent,
    inner_got,
    cross_ref,
    v_ref,
    cv_ref,
    w_ref,
    q_ref,
    left_ref,
    out_hbm,
    fix_ref,
    mix_vm,
    out_vm,
    sems,
):
    del left_in, left_ref

    @pl.when(lax.axis_index("sub") == 0)
    def _():
        def keep_fix(k, i, plane):
            fix_ref[k, eight(i), :] = plane

        stores = finish_half(
            1,
            lambda slab, lanes: right_sent[slab, :, lanes],
            lambda slab, lanes: inner_got[slab, :, lanes],
            cross_ref,
            v_ref,
            cv_ref,
            w_ref,
            q_ref,
            mix_vm,
            out_vm,
            out_hbm,
            sems,
            keep_fix,
        )
        for store in stores:
            store.wait()


def lower_kernel(
    out_in,
    upper_fix,
    left_sent,
    right_got,
    cross_ref,
    v_ref,
    cv_ref,
    w_ref,
    q_ref,
    out_hbm,
    fix_hbm,
    mix_vm,
    out_vm,
    sems,
    fix_vm,
    fix_sem,
):
    del out_in

    @pl.when(lax.axis_index("sub") == 0)
    def _():
        def keep_fix(k, i, plane):
            fix_vm[k, pl.ds(i, 8, 8), :] = plane

        for k in range(COMPS):
            for i in range(4):
                fix_vm[k, pl.ds(4 + i, 8, 8), :] = upper_fix[k, eight(i), :]
        stores = finish_half(
            0,
            lambda slab, lanes: left_sent[slab, :, lanes],
            lambda slab, lanes: right_got[slab, :, lanes],
            cross_ref,
            v_ref,
            cv_ref,
            w_ref,
            q_ref,
            mix_vm,
            out_vm,
            out_hbm,
            sems,
            keep_fix,
        )
        fix_copy = pltpu.make_async_copy(fix_vm, fix_hbm, fix_sem)
        fix_copy.start()
        for store in stores:
            store.wait()
        fix_copy.wait()


def finish_kernel(
    out_in,
    fix_in,
    left_sent,
    right_sent,
    right_got,
    inner_got,
    outer_got,
    cross_ref,
    v_ref,
    cv_ref,
    w_ref,
    q_ref,
    out_hbm,
    fix_hbm,
    mix_vm,
    out_vm,
    sems,
    fix_vm,
    fix_sem,
):
    del out_in, fix_in
    at = lax.axis_index("sub")
    inner = at < lax.axis_size("sub") - 2

    def left_got(slab, lanes):
        return jnp.where(inner, inner_got[slab, :, lanes], outer_got[slab, :, lanes])

    def half(which, sent, got):
        def keep_fix(k, i, plane):
            fix_vm[k, pl.ds(4 * which + i, 8, 8), :] = plane

        refs = (cross_ref, v_ref, cv_ref, w_ref, q_ref, mix_vm, out_vm, out_hbm, sems, keep_fix)
        return finish_half(which, lambda slab, lanes: sent[slab, :, lanes], got, *refs)

    @pl.when(at != 0)
    def _():
        stores = half(0, left_sent, lambda slab, lanes: right_got[slab, :, lanes])
        stores += half(1, right_sent, left_got)
        fix_copy = pltpu.make_async_copy(fix_vm, fix_hbm, fix_sem)
        fix_copy.start()
        for store in stores:
            store.wait()
        fix_copy.wait()


VMEM = pl.BlockSpec(memory_space=pltpu.VMEM)
HBM = pl.BlockSpec(memory_space=pltpu.HBM)
ANY = pl.BlockSpec(memory_space=pl.ANY)
PARAMS = pltpu.CompilerParams(vmem_limit_bytes=16 * 2**20)
FINE_TILED = (2, 8 * TILES, LANES)


def fine_tiled(field):
    lead = field.shape[:-2]
    split = field.reshape(lead + (2, 8, TILES, LANES))
    return jnp.swapaxes(split, -3, -2).reshape(lead + FINE_TILED)


def pinned(field):
    return pltpu.with_memory_space_constraint(field, pltpu.HBM)


def shards(velocity, forcing, viscosity, coarse_visc):
    coeffs = jnp.swapaxes(coarse_visc.reshape(HALF, BLOCKS, LANES), 0, 1).reshape(8 * HALF, LANES)
    message = jax.ShapeDtypeStruct((7, 8, WIDE), F32)
    fine = jax.ShapeDtypeStruct((COMPS,) + FINE_TILED, F32)
    coarse = jax.ShapeDtypeStruct((COMPS, 8 * HALF, LANES), F32)
    crosses = jax.ShapeDtypeStruct((COMPS, 8 * PLANES, LANES), F32)
    right_sent, left_sent, cross, *kept = pl.pallas_call(
        local_kernel,
        out_shape=(
            message,
            message,
            crosses,
            fine,
            jax.ShapeDtypeStruct((8 * HALF, LANES), F32),
            jax.ShapeDtypeStruct((WIDE, 2 * LANES), BF16),
            jax.ShapeDtypeStruct((2 * LANES, WIDE), BF16),
        ),
        in_specs=[HBM] * 4,
        out_specs=(VMEM,) * 7,
        scratch_shapes=[
            pltpu.VMEM((COMPS,) + FINE_TILED, F32),
            pltpu.VMEM(FINE_TILED, F32),
            pltpu.VMEM((2, COMPS * BLOCKS * PLANES, WIDE), BF16),
            pltpu.SemaphoreType.DMA((2 + 2 * COMPS,)),
        ],
        compiler_params=PARAMS,
    )(
        pinned(fine_tiled(velocity)),
        pinned(fine_tiled(forcing)),
        pinned(fine_tiled(viscosity)),
        pinned(coeffs),
    )

    axes = ("grp", "sub")
    count, deep = lax.axis_size(axes), lax.axis_size("sub")
    inner = [(i + 1, i) for i in range(count - 1) if i % deep < deep - 2]
    outer = [(i + 1, i) for i in range(count - 1) if i % deep >= deep - 2]
    right_got = lax.ppermute(right_sent, axes, [(i, i + 1) for i in range(count - 1)])
    inner_got = lax.ppermute(left_sent, axes, inner)
    half_scratch = [
        pltpu.VMEM((COMPS, 8 * 8, LANES), F32),
        pltpu.VMEM((COMPS,) + FINE_TILED, F32),
    ]
    left_sent, corrected, upper_fix = pl.pallas_call(
        upper_kernel,
        out_shape=(message, fine, jax.ShapeDtypeStruct((COMPS, 4 * 8, LANES), F32)),
        in_specs=[ANY] + [VMEM] * 7,
        out_specs=(ANY, HBM, VMEM),
        input_output_aliases={0: 0},
        scratch_shapes=half_scratch + [pltpu.SemaphoreType.DMA((COMPS, 2))],
        compiler_params=PARAMS,
    )(left_sent, right_sent, inner_got, cross, *kept)
    outer_got = lax.ppermute(left_sent, axes, outer)
    finish_scratch = half_scratch + [
        pltpu.SemaphoreType.DMA((COMPS, 2)),
        pltpu.VMEM((COMPS, 8 * HALF, LANES), F32),
        pltpu.SemaphoreType.DMA,
    ]
    corrected, fix = pl.pallas_call(
        lower_kernel,
        out_shape=(fine, coarse),
        in_specs=[HBM] + [VMEM] * 8,
        out_specs=(HBM, HBM),
        input_output_aliases={0: 0},
        scratch_shapes=finish_scratch,
        compiler_params=PARAMS,
    )(pinned(corrected), upper_fix, left_sent, right_got, cross, *kept)
    corrected, fix = pl.pallas_call(
        finish_kernel,
        out_shape=(fine, coarse),
        in_specs=[HBM, HBM] + [VMEM] * 10,
        out_specs=(HBM, HBM),
        input_output_aliases={0: 0, 1: 1},
        scratch_shapes=finish_scratch,
        compiler_params=PARAMS,
    )(
        pinned(corrected),
        pinned(fix),
        left_sent,
        right_sent,
        right_got,
        inner_got,
        outer_got,
        cross,
        *kept,
    )
    corrected = corrected.reshape(COMPS, 2, TILES, 8, LANES)
    fix = fix.reshape(COMPS, BLOCKS, HALF, LANES)
    return (
        jnp.swapaxes(corrected, 2, 3).reshape(velocity.shape),
        jnp.swapaxes(fix, 1, 2).reshape(COMPS, HALF, COARSE),
    )


def solution(mesh):
    return jax.shard_map(
        shards,
        mesh=mesh,
        in_specs=(
            P(None, ("grp", "sub"), None),
            P(None, ("grp", "sub"), None),
            P(("grp", "sub"), None),
            P(("grp", "sub"), None),
        ),
        out_specs=(P(None, ("grp", "sub"), None), P(None, ("grp", "sub"), None)),
        check_vma=False,
    )
```

```python
import jax
import jax.numpy as jnp
from jax import lax
from jax.experimental import pallas as pl
from jax.experimental.pallas import tpu as pltpu
from jax.sharding import PartitionSpec as P

NY = 32
NZ = 32
DEGREE = 3
LOWER_EIG = 0.15
UPPER_EIG = 1.95
CENTER = 0.5 * (UPPER_EIG + LOWER_EIG)
HALF_WIDTH = 0.5 * (UPPER_EIG - LOWER_EIG)

COMPS = 3
FINE = 4 * NY * NZ
COARSE = NY * NZ
PLANES = 16
HALF = PLANES // 2
LANES = 128
BLOCKS = COARSE // LANES
WIDE = FINE // BLOCKS
TILES = FINE // LANES
F32 = jnp.float32
BF16 = jnp.bfloat16


def tile(index):
    return slice(LANES * index, LANES * (index + 1))


def fill_restrict(ref):
    fine = lax.broadcasted_iota(jnp.int32, (2 * NZ, LANES), 0)
    lane = lax.broadcasted_iota(jnp.int32, (2 * NZ, LANES), 1)
    apart = (fine - 2 * (lane % NZ) + 2 * NZ) % (2 * NZ)
    cols = jnp.where(apart == 0, 1.0, jnp.where((apart == 1) | (apart == 2 * NZ - 1), 0.5, 0.0))
    for row in range(8):
        away = jnp.abs(2 * (lane // NZ) - row)
        rows = jnp.where(away == 0, 1.0, jnp.where(away == 1, 0.5, 0.0))
        at = slice(2 * NZ * row, 2 * NZ * (row + 1))
        ref[at, :LANES] = (cols * rows).astype(BF16)
        beyond = jnp.where(lane < NZ, 0.5 * cols, 0.0) if row == 7 else jnp.zeros_like(cols)
        ref[at, LANES:] = beyond.astype(BF16)


def fill_prolong(ref):
    coarse = lax.broadcasted_iota(jnp.int32, (NZ, LANES), 0)
    lane = lax.broadcasted_iota(jnp.int32, (NZ, LANES), 1)
    apart = (lane - 2 * coarse + 2 * NZ) % (2 * NZ)
    cols = jnp.where(apart == 0, 1.0, jnp.where((apart == 1) | (apart == 2 * NZ - 1), 0.5, 0.0))
    for row in range(8):
        for part in range(4):
            away = jnp.abs(2 * row - 2 * part - lane // (2 * NZ))
            rows = jnp.where(away == 0, 1.0, jnp.where(away == 1, 0.5, 0.0))
            kept = cols * rows if row < 5 else jnp.zeros_like(cols)
            ref[NZ * row : NZ * (row + 1), tile(part)] = kept.astype(BF16)


def halves(values):
    high = values.astype(BF16)
    return high, (values - high.astype(F32)).astype(BF16)


def split_dot(left, matrix):
    rows = left.shape[0]
    sums = jnp.dot(jnp.concatenate(halves(left), axis=0), matrix, preferred_element_type=F32)
    return sums[:rows] + sums[rows:]


def iotas(rows):
    row = lax.broadcasted_iota(jnp.int32, (rows, LANES), 0)
    lane = lax.broadcasted_iota(jnp.int32, (rows, LANES), 1)
    return row, lane


def eight(index):
    return slice(8 * index, 8 * (index + 1))


def local_kernel(
    v_hbm,
    f_hbm,
    c_hbm,
    cv_hbm,
    right_ref,
    left_ref,
    cross_ref,
    v_ref,
    cv_ref,
    w_ref,
    q_ref,
    f_vm,
    c_vm,
    split_vm,
    beside_vm,
    sems,
):
    c_copy = pltpu.make_async_copy(c_hbm, c_vm, sems.at[0])
    cv_copy = pltpu.make_async_copy(cv_hbm, cv_ref, sems.at[1])
    v_copies, f_copies = [], []
    for k in range(COMPS):
        v_copies.append(pltpu.make_async_copy(v_hbm.at[k], v_ref.at[k], sems.at[2 + 2 * k]))
        f_copies.append(pltpu.make_async_copy(f_hbm.at[k], f_vm.at[k], sems.at[3 + 2 * k]))
    v_copies[0].start()
    c_copy.start()
    for k in range(COMPS):
        if k > 0:
            v_copies[k].start()
        f_copies[k].start()
    cv_copy.start()

    row, lane = iotas(PLANES)
    low_half = lane < 64
    first_col = lane % 64 == 0
    last_col = lane % 64 == 63
    fill_restrict(w_ref)
    fill_prolong(q_ref)

    def packed_planes(slab, source):
        for part in range(4):
            left_ref[slab, :, tile(part)] = source[0, pl.ds(8 * part, 8, 32), :]
            right_ref[slab, :, tile(part)] = source[1, pl.ds(8 * part + 7, 8, 32), :]

    for k in range(COMPS):
        v_copies[k].wait()

        def planes_of(ref, t):
            return jnp.concatenate([ref[0, eight(t), :], ref[1, eight(t), :]], axis=0)

        values = [planes_of(v_ref.at[k], t) for t in range(TILES)]
        swapped = [pltpu.roll(x, 64, 1) for x in values]
        for t in range(TILES):
            x, turned = values[t], swapped[t]
            beside = turned + jnp.where(low_half, swapped[t - 1], swapped[(t + 1) % TILES])
            beside += pltpu.roll(jnp.where(last_col, turned, x), 1, 1)
            beside += pltpu.roll(jnp.where(first_col, turned, x), LANES - 1, 1)
            beside += jnp.where(row == 0, 0.0, pltpu.roll(x, 1, 0))
            beside += jnp.where(row == PLANES - 1, 0.0, pltpu.roll(x, PLANES - 1, 0))
            beside_vm[t] = beside - 6.0 * x
        if k == 0:
            c_copy.wait()
            packed_planes(COMPS, c_vm)
        f_copies[k].wait()
        for t in range(TILES):
            scaled = planes_of(c_vm, t) * beside_vm[t]
            residual = planes_of(f_vm.at[k], t) - planes_of(v_ref.at[k], t) + scaled
            first = PLANES * (BLOCKS * k + t // 4)
            for part, value in enumerate(halves(residual)):
                split_vm[part, first : first + PLANES, tile(t % 4)] = value

    matrix = w_ref[...]
    sums = jnp.dot(split_vm[0], matrix, preferred_element_type=F32)
    sums += jnp.dot(split_vm[1], matrix, preferred_element_type=F32)
    for k in range(COMPS):
        mine = sums[PLANES * BLOCKS * k : PLANES * BLOCKS * (k + 1)]
        parts = [mine[PLANES * s : PLANES * (s + 1)] for s in range(BLOCKS)]
        for s in range(BLOCKS):
            crossed = parts[s][:, :LANES] + parts[s - 1][:, LANES:]
            cross_ref[k, PLANES * s : PLANES * (s + 1), :] = crossed
    for k in range(COMPS):
        planes = [cross_ref[k, pl.ds(p, 8, PLANES), :] for p in range(PLANES)]
        half_odds = [0.0625 * planes[2 * j + 1] for j in range(HALF)]
        sources = []
        for j in range(HALF):
            source = 0.125 * planes[2 * j] + half_odds[j]
            if j > 0:
                source += half_odds[j - 1]
            sources.append(source)
        for j in range(3):
            left_ref[4 + j, :, tile(k)] = sources[j]
            right_ref[4 + j, :, tile(k)] = (sources[6:] + half_odds[-1:])[j]
        packed_planes(k, v_ref.at[k])

    cv_copy.wait()
    for j in range(3):
        left_ref[4 + j, :, tile(COMPS)] = cv_ref[pl.ds(j, 8, 8), :]
        right_ref[4 + j, :, tile(COMPS)] = cv_ref[pl.ds(min(6 + j, 7), 8, 8), :]


def finish_half(h, sent, got, cross_ref, v_ref, cv_ref, w_ref, q_ref, mix_vm, out_vm, out_hbm, sems, keep_fix):
    _, lane = iotas(8)
    kept_up = lane < LANES - NZ
    kept_down = lane >= NZ
    first_col = lane % NZ == 0
    last_col = lane % NZ == NZ - 1
    whole = slice(0, WIDE)

    their_coeff, own_coeff = got(COMPS, whole), sent(COMPS, whole)
    rows = [got(k, whole) * own_coeff for k in range(COMPS)]
    rows += [sent(k, whole) * their_coeff for k in range(COMPS)]
    sums = split_dot(jnp.concatenate(rows, axis=0), w_ref[...])
    terms = []
    for part in range(2 * COMPS):
        mine = sums[eight(part)]
        terms.append(mine[:, :LANES] + pltpu.roll(mine[:, LANES:], 1, 0))

    first = 4 * h - 2
    last = first + 8
    inverse, quotient = {}, {}
    for j in range(first, last + 1):
        if j < 0:
            coeff = got(6 + j, tile(COMPS))
        elif j < HALF:
            coeff = cv_ref[pl.ds(j, 8, 8), :]
        else:
            coeff = got(4 + j - HALF, tile(COMPS))
        if j == HALF:
            inside = coeff > 0.0
        inverse[j] = 1.0 / (1.0 + 6.0 * coeff)
        quotient[j] = coeff * inverse[j]

    def near_sum(planes, j):
        x = planes[j]
        up = pltpu.roll(x, LANES - NZ, 1)
        down = pltpu.roll(x, NZ, 1)
        total = planes[j - 1] + planes[j + 1]
        total += jnp.where(kept_up, up, pltpu.roll(up, 7, 0))
        total += jnp.where(kept_down, down, pltpu.roll(down, 1, 0))
        total += pltpu.roll(jnp.where(last_col, up, x), 1, 1)
        total += pltpu.roll(jnp.where(first_col, down, x), LANES - 1, 1)
        return total

    sigma = CENTER / HALF_WIDTH
    for k in range(COMPS):
        at = tile(k)
        theirs, ours = terms[k], terms[COMPS + k]

        def crossed(p):
            return cross_ref[k, pl.ds(p, 8, PLANES), :]

        source = {}
        for j in range(max(first, 0), min(last, HALF - 1) + 1):
            beside = crossed(2 * j + 1)
            if j > 0:
                beside += crossed(2 * j - 1)
            source[j] = 0.125 * crossed(2 * j) + 0.0625 * beside
        if h == 0:
            source[-2] = got(4, at)
            source[-1] = got(5, at) + 0.0625 * ours
            source[0] += got(6, at) + (0.125 * theirs + 0.0625 * ours)
        else:
            source[HALF - 1] += 0.0625 * theirs
            after = sent(6, at) + got(4, at) + (0.0625 * theirs + 0.125 * ours)
            source[HALF] = jnp.where(inside, after, 0.0)
            source[HALF + 1] = got(5, at)
            source[HALF + 2] = got(6, at)

        scaled = {j: source[j] * inverse[j] for j in source}
        update = {j: x * (1.0 / CENTER) for j, x in scaled.items()}
        approx = update
        ratio_old = 1.0 / sigma
        for sweep in range(1, DEGREE):
            ratio_new = 1.0 / (2.0 * sigma - ratio_old)
            keep, gain = ratio_new * ratio_old, 2.0 * ratio_new / HALF_WIDTH
            inner = range(first + sweep, last - sweep + 1)
            update = {
                j: keep * update[j]
                + gain * (scaled[j] - approx[j] + quotient[j] * near_sum(approx, j))
                for j in inner
            }
            approx = {j: approx[j] + update[j] for j in inner}
            ratio_old = ratio_new

        for i in range(4):
            here, after = approx[4 * h + i], approx[4 * h + i + 1]
            keep_fix(k, i, here)
            mix_vm[k, eight(2 * i), :] = here
            mix_vm[k, eight(2 * i + 1), :] = 0.5 * (here + after)
    left = []
    for k in range(COMPS):
        mixed = [mix_vm[k, pl.ds(s, 8, 8), :] for s in range(BLOCKS)]
        left += [
            jnp.concatenate([mixed[s], mixed[(s + 1) % BLOCKS]], axis=1) for s in range(BLOCKS)
        ]
    fine = split_dot(jnp.concatenate(left, axis=0), q_ref[...])
    stores = []
    for k in range(COMPS):
        for t in range(TILES):
            add = fine[eight(BLOCKS * k + t // 4), tile(t % 4)]
            out_vm[k, h, eight(t), :] = v_ref[k, h, eight(t), :] + add
        store = pltpu.make_async_copy(out_vm.at[k, h], out_hbm.at[k, h], sems.at[k, h])
        store.start()
        stores.append(store)
    return stores


def upper_kernel(
    left_in,
    right_sent,
    inner_got,
    cross_ref,
    v_ref,
    cv_ref,
    w_ref,
    q_ref,
    left_ref,
    out_hbm,
    fix_ref,
    mix_vm,
    out_vm,
    sems,
):
    del left_in, left_ref

    @pl.when(lax.axis_index("sub") == 0)
    def _():
        def keep_fix(k, i, plane):
            fix_ref[k, eight(i), :] = plane

        stores = finish_half(
            1,
            lambda slab, lanes: right_sent[slab, :, lanes],
            lambda slab, lanes: inner_got[slab, :, lanes],
            cross_ref,
            v_ref,
            cv_ref,
            w_ref,
            q_ref,
            mix_vm,
            out_vm,
            out_hbm,
            sems,
            keep_fix,
        )
        for store in stores:
            store.wait()


def lower_kernel(
    out_in,
    upper_fix,
    left_sent,
    right_got,
    cross_ref,
    v_ref,
    cv_ref,
    w_ref,
    q_ref,
    out_hbm,
    fix_hbm,
    mix_vm,
    out_vm,
    sems,
    fix_vm,
    fix_sem,
):
    del out_in

    @pl.when(lax.axis_index("sub") == 0)
    def _():
        def keep_fix(k, i, plane):
            fix_vm[k, pl.ds(i, 8, 8), :] = plane

        for k in range(COMPS):
            for i in range(4):
                fix_vm[k, pl.ds(4 + i, 8, 8), :] = upper_fix[k, eight(i), :]
        stores = finish_half(
            0,
            lambda slab, lanes: left_sent[slab, :, lanes],
            lambda slab, lanes: right_got[slab, :, lanes],
            cross_ref,
            v_ref,
            cv_ref,
            w_ref,
            q_ref,
            mix_vm,
            out_vm,
            out_hbm,
            sems,
            keep_fix,
        )
        fix_copy = pltpu.make_async_copy(fix_vm, fix_hbm, fix_sem)
        fix_copy.start()
        for store in stores:
            store.wait()
        fix_copy.wait()


def finish_kernel(
    out_in,
    fix_in,
    left_sent,
    right_sent,
    right_got,
    inner_got,
    outer_got,
    cross_ref,
    v_ref,
    cv_ref,
    w_ref,
    q_ref,
    out_hbm,
    fix_hbm,
    mix_vm,
    out_vm,
    sems,
    fix_vm,
    fix_sem,
):
    del out_in, fix_in
    at = lax.axis_index("sub")
    inner = at < lax.axis_size("sub") - 2

    def left_got(slab, lanes):
        return jnp.where(inner, inner_got[slab, :, lanes], outer_got[slab, :, lanes])

    def half(which, sent, got):
        def keep_fix(k, i, plane):
            fix_vm[k, pl.ds(4 * which + i, 8, 8), :] = plane

        refs = (cross_ref, v_ref, cv_ref, w_ref, q_ref, mix_vm, out_vm, out_hbm, sems, keep_fix)
        return finish_half(which, lambda slab, lanes: sent[slab, :, lanes], got, *refs)

    @pl.when(at != 0)
    def _():
        stores = half(0, left_sent, lambda slab, lanes: right_got[slab, :, lanes])
        stores += half(1, right_sent, left_got)
        fix_copy = pltpu.make_async_copy(fix_vm, fix_hbm, fix_sem)
        fix_copy.start()
        for store in stores:
            store.wait()
        fix_copy.wait()


VMEM = pl.BlockSpec(memory_space=pltpu.VMEM)
HBM = pl.BlockSpec(memory_space=pltpu.HBM)
ANY = pl.BlockSpec(memory_space=pl.ANY)
PARAMS = pltpu.CompilerParams(vmem_limit_bytes=16 * 2**20)
FINE_TILED = (2, 8 * TILES, LANES)


def fine_tiled(field):
    lead = field.shape[:-2]
    split = field.reshape(lead + (2, 8, TILES, LANES))
    return jnp.swapaxes(split, -3, -2).reshape(lead + FINE_TILED)


def pinned(field):
    return pltpu.with_memory_space_constraint(field, pltpu.HBM)


def shards(velocity, forcing, viscosity, coarse_visc):
    coeffs = jnp.swapaxes(coarse_visc.reshape(HALF, BLOCKS, LANES), 0, 1).reshape(8 * HALF, LANES)
    message = jax.ShapeDtypeStruct((7, 8, WIDE), F32)
    fine = jax.ShapeDtypeStruct((COMPS,) + FINE_TILED, F32)
    coarse = jax.ShapeDtypeStruct((COMPS, 8 * HALF, LANES), F32)
    crosses = jax.ShapeDtypeStruct((COMPS, 8 * PLANES, LANES), F32)
    right_sent, left_sent, cross, *kept = pl.pallas_call(
        local_kernel,
        out_shape=(
            message,
            message,
            crosses,
            fine,
            jax.ShapeDtypeStruct((8 * HALF, LANES), F32),
            jax.ShapeDtypeStruct((WIDE, 2 * LANES), BF16),
            jax.ShapeDtypeStruct((2 * LANES, WIDE), BF16),
        ),
        in_specs=[HBM] * 4,
        out_specs=(VMEM,) * 7,
        scratch_shapes=[
            pltpu.VMEM((COMPS,) + FINE_TILED, F32),
            pltpu.VMEM(FINE_TILED, F32),
            pltpu.VMEM((2, COMPS * BLOCKS * PLANES, WIDE), BF16),
            pltpu.VMEM((TILES, PLANES, LANES), F32),
            pltpu.SemaphoreType.DMA((2 + 2 * COMPS,)),
        ],
        compiler_params=PARAMS,
    )(
        pinned(fine_tiled(velocity)),
        pinned(fine_tiled(forcing)),
        pinned(fine_tiled(viscosity)),
        pinned(coeffs),
    )

    axes = ("grp", "sub")
    count, deep = lax.axis_size(axes), lax.axis_size("sub")
    inner = [(i + 1, i) for i in range(count - 1) if i % deep < deep - 2]
    outer = [(i + 1, i) for i in range(count - 1) if i % deep >= deep - 2]
    right_got = lax.ppermute(right_sent, axes, [(i, i + 1) for i in range(count - 1)])
    inner_got = lax.ppermute(left_sent, axes, inner)
    half_scratch = [
        pltpu.VMEM((COMPS, 8 * 8, LANES), F32),
        pltpu.VMEM((COMPS,) + FINE_TILED, F32),
    ]
    left_sent, corrected, upper_fix = pl.pallas_call(
        upper_kernel,
        out_shape=(message, fine, jax.ShapeDtypeStruct((COMPS, 4 * 8, LANES), F32)),
        in_specs=[ANY] + [VMEM] * 7,
        out_specs=(ANY, HBM, VMEM),
        input_output_aliases={0: 0},
        scratch_shapes=half_scratch + [pltpu.SemaphoreType.DMA((COMPS, 2))],
        compiler_params=PARAMS,
    )(left_sent, right_sent, inner_got, cross, *kept)
    outer_got = lax.ppermute(left_sent, axes, outer)
    finish_scratch = half_scratch + [
        pltpu.SemaphoreType.DMA((COMPS, 2)),
        pltpu.VMEM((COMPS, 8 * HALF, LANES), F32),
        pltpu.SemaphoreType.DMA,
    ]
    corrected, fix = pl.pallas_call(
        lower_kernel,
        out_shape=(fine, coarse),
        in_specs=[HBM] + [VMEM] * 8,
        out_specs=(HBM, HBM),
        input_output_aliases={0: 0},
        scratch_shapes=finish_scratch,
        compiler_params=PARAMS,
    )(pinned(corrected), upper_fix, left_sent, right_got, cross, *kept)
    corrected, fix = pl.pallas_call(
        finish_kernel,
        out_shape=(fine, coarse),
        in_specs=[HBM, HBM] + [VMEM] * 10,
        out_specs=(HBM, HBM),
        input_output_aliases={0: 0, 1: 1},
        scratch_shapes=finish_scratch,
        compiler_params=PARAMS,
    )(
        pinned(corrected),
        pinned(fix),
        left_sent,
        right_sent,
        right_got,
        inner_got,
        outer_got,
        cross,
        *kept,
    )
    corrected = corrected.reshape(COMPS, 2, TILES, 8, LANES)
    fix = fix.reshape(COMPS, BLOCKS, HALF, LANES)
    return (
        jnp.swapaxes(corrected, 2, 3).reshape(velocity.shape),
        jnp.swapaxes(fix, 1, 2).reshape(COMPS, HALF, COARSE),
    )


def solution(mesh):
    return jax.shard_map(
        shards,
        mesh=mesh,
        in_specs=(
            P(None, ("grp", "sub"), None),
            P(None, ("grp", "sub"), None),
            P(("grp", "sub"), None),
            P(("grp", "sub"), None),
        ),
        out_specs=(P(None, ("grp", "sub"), None), P(None, ("grp", "sub"), None)),
        check_vma=False,
    )
```

```python
import jax
import jax.numpy as jnp
from jax import lax
from jax.experimental import pallas as pl
from jax.experimental.pallas import tpu as pltpu
from jax.sharding import PartitionSpec as P

NY = 32
NZ = 32
DEGREE = 3
LOWER_EIG = 0.15
UPPER_EIG = 1.95
CENTER = 0.5 * (UPPER_EIG + LOWER_EIG)
HALF_WIDTH = 0.5 * (UPPER_EIG - LOWER_EIG)

COMPS = 3
FINE = 4 * NY * NZ
COARSE = NY * NZ
PLANES = 16
HALF = PLANES // 2
LANES = 128
BLOCKS = COARSE // LANES
WIDE = FINE // BLOCKS
TILES = FINE // LANES
F32 = jnp.float32
BF16 = jnp.bfloat16


def tile(index):
    return slice(LANES * index, LANES * (index + 1))


def fill_restrict(ref):
    fine = lax.broadcasted_iota(jnp.int32, (2 * NZ, LANES), 0)
    lane = lax.broadcasted_iota(jnp.int32, (2 * NZ, LANES), 1)
    apart = (fine - 2 * (lane % NZ) + 2 * NZ) % (2 * NZ)
    cols = jnp.where(apart == 0, 1.0, jnp.where((apart == 1) | (apart == 2 * NZ - 1), 0.5, 0.0))
    for row in range(8):
        away = jnp.abs(2 * (lane // NZ) - row)
        rows = jnp.where(away == 0, 1.0, jnp.where(away == 1, 0.5, 0.0))
        at = slice(2 * NZ * row, 2 * NZ * (row + 1))
        ref[at, :LANES] = (cols * rows).astype(BF16)
        beyond = jnp.where(lane < NZ, 0.5 * cols, 0.0) if row == 7 else jnp.zeros_like(cols)
        ref[at, LANES:] = beyond.astype(BF16)


def fill_prolong(ref):
    coarse = lax.broadcasted_iota(jnp.int32, (NZ, LANES), 0)
    lane = lax.broadcasted_iota(jnp.int32, (NZ, LANES), 1)
    apart = (lane - 2 * coarse + 2 * NZ) % (2 * NZ)
    cols = jnp.where(apart == 0, 1.0, jnp.where((apart == 1) | (apart == 2 * NZ - 1), 0.5, 0.0))
    for row in range(8):
        for part in range(4):
            away = jnp.abs(2 * row - 2 * part - lane // (2 * NZ))
            rows = jnp.where(away == 0, 1.0, jnp.where(away == 1, 0.5, 0.0))
            kept = cols * rows if row < 5 else jnp.zeros_like(cols)
            ref[NZ * row : NZ * (row + 1), tile(part)] = kept.astype(BF16)


def halves(values):
    high = values.astype(BF16)
    return high, (values - high.astype(F32)).astype(BF16)


def split_dot(left, matrix):
    rows = left.shape[0]
    sums = jnp.dot(jnp.concatenate(halves(left), axis=0), matrix, preferred_element_type=F32)
    return sums[:rows] + sums[rows:]


def iotas(rows):
    row = lax.broadcasted_iota(jnp.int32, (rows, LANES), 0)
    lane = lax.broadcasted_iota(jnp.int32, (rows, LANES), 1)
    return row, lane


def eight(index):
    return slice(8 * index, 8 * (index + 1))


def local_kernel(
    v_hbm,
    f_hbm,
    c_hbm,
    cv_hbm,
    right_ref,
    left_ref,
    cross_ref,
    v_ref,
    cv_ref,
    w_ref,
    q_ref,
    f_vm,
    c_vm,
    split_vm,
    sems,
):
    copies = [pltpu.make_async_copy(c_hbm, c_vm, sems.at[0])]
    for k in range(COMPS):
        copies.append(pltpu.make_async_copy(v_hbm.at[k], v_ref.at[k], sems.at[1 + 2 * k]))
        copies.append(pltpu.make_async_copy(f_hbm.at[k], f_vm.at[k], sems.at[2 + 2 * k]))
    copies.append(pltpu.make_async_copy(cv_hbm, cv_ref, sems.at[1 + 2 * COMPS]))
    for copy in copies:
        copy.start()

    row, lane = iotas(PLANES)
    low_half = lane < 64
    first_col = lane % 64 == 0
    last_col = lane % 64 == 63
    fill_restrict(w_ref)
    fill_prolong(q_ref)

    def packed_planes(slab, source):
        for part in range(4):
            left_ref[slab, :, tile(part)] = source[0, pl.ds(8 * part, 8, 32), :]
            right_ref[slab, :, tile(part)] = source[1, pl.ds(8 * part + 7, 8, 32), :]

    copies[0].wait()
    packed_planes(COMPS, c_vm)

    for k in range(COMPS):
        copies[1 + 2 * k].wait()
        copies[2 + 2 * k].wait()
        packed_planes(k, v_ref.at[k])

        def planes_of(ref, t):
            return jnp.concatenate([ref[0, eight(t), :], ref[1, eight(t), :]], axis=0)

        values = [planes_of(v_ref.at[k], t) for t in range(TILES)]
        swapped = [pltpu.roll(x, 64, 1) for x in values]
        for s in range(BLOCKS):
            at = slice(PLANES * (BLOCKS * k + s), PLANES * (BLOCKS * k + s + 1))
            for t in range(4 * s, 4 * s + 4):
                x, turned = values[t], swapped[t]
                beside = turned + jnp.where(low_half, swapped[t - 1], swapped[(t + 1) % TILES])
                beside += pltpu.roll(jnp.where(last_col, turned, x), 1, 1)
                beside += pltpu.roll(jnp.where(first_col, turned, x), LANES - 1, 1)
                beside += jnp.where(row == 0, 0.0, pltpu.roll(x, 1, 0))
                beside += jnp.where(row == PLANES - 1, 0.0, pltpu.roll(x, PLANES - 1, 0))
                residual = planes_of(f_vm.at[k], t) - x + planes_of(c_vm, t) * (beside - 6.0 * x)
                for part, value in enumerate(halves(residual)):
                    split_vm[part, at, tile(t % 4)] = value

    matrix = w_ref[...]
    sums = jnp.dot(split_vm[0], matrix, preferred_element_type=F32)
    sums += jnp.dot(split_vm[1], matrix, preferred_element_type=F32)
    for k in range(COMPS):
        mine = sums[PLANES * BLOCKS * k : PLANES * BLOCKS * (k + 1)]
        parts = [mine[PLANES * s : PLANES * (s + 1)] for s in range(BLOCKS)]
        for s in range(BLOCKS):
            crossed = parts[s][:, :LANES] + parts[s - 1][:, LANES:]
            cross_ref[k, PLANES * s : PLANES * (s + 1), :] = crossed
    for k in range(COMPS):
        planes = [cross_ref[k, pl.ds(p, 8, PLANES), :] for p in range(PLANES)]
        half_odds = [0.0625 * planes[2 * j + 1] for j in range(HALF)]
        sources = []
        for j in range(HALF):
            source = 0.125 * planes[2 * j] + half_odds[j]
            if j > 0:
                source += half_odds[j - 1]
            sources.append(source)
        for j in range(3):
            left_ref[4 + j, :, tile(k)] = sources[j]
            right_ref[4 + j, :, tile(k)] = (sources[6:] + half_odds[-1:])[j]

    copies[-1].wait()
    for j in range(3):
        left_ref[4 + j, :, tile(COMPS)] = cv_ref[pl.ds(j, 8, 8), :]
        right_ref[4 + j, :, tile(COMPS)] = cv_ref[pl.ds(min(6 + j, 7), 8, 8), :]


def finish_half(h, sent, got, cross_ref, v_ref, cv_ref, w_ref, q_ref, mix_vm, out_vm, out_hbm, sems, keep_fix):
    _, lane = iotas(8)
    kept_up = lane < LANES - NZ
    kept_down = lane >= NZ
    first_col = lane % NZ == 0
    last_col = lane % NZ == NZ - 1
    whole = slice(0, WIDE)

    their_coeff, own_coeff = got(COMPS, whole), sent(COMPS, whole)
    rows = [got(k, whole) * own_coeff for k in range(COMPS)]
    rows += [sent(k, whole) * their_coeff for k in range(COMPS)]
    sums = split_dot(jnp.concatenate(rows, axis=0), w_ref[...])
    terms = []
    for part in range(2 * COMPS):
        mine = sums[eight(part)]
        terms.append(mine[:, :LANES] + pltpu.roll(mine[:, LANES:], 1, 0))

    first = 4 * h - 2
    last = first + 8
    inverse, quotient = {}, {}
    for j in range(first, last + 1):
        if j < 0:
            coeff = got(6 + j, tile(COMPS))
        elif j < HALF:
            coeff = cv_ref[pl.ds(j, 8, 8), :]
        else:
            coeff = got(4 + j - HALF, tile(COMPS))
        if j == HALF:
            inside = coeff > 0.0
        inverse[j] = 1.0 / (1.0 + 6.0 * coeff)
        quotient[j] = coeff * inverse[j]

    def near_sum(planes, j):
        x = planes[j]
        up = pltpu.roll(x, LANES - NZ, 1)
        down = pltpu.roll(x, NZ, 1)
        total = planes[j - 1] + planes[j + 1]
        total += jnp.where(kept_up, up, pltpu.roll(up, 7, 0))
        total += jnp.where(kept_down, down, pltpu.roll(down, 1, 0))
        total += jnp.where(first_col, pltpu.roll(x, LANES - NZ + 1, 1), pltpu.roll(x, 1, 1))
        total += jnp.where(last_col, pltpu.roll(x, NZ - 1, 1), pltpu.roll(x, LANES - 1, 1))
        return total

    sigma = CENTER / HALF_WIDTH
    for k in range(COMPS):
        at = tile(k)
        theirs, ours = terms[k], terms[COMPS + k]

        def crossed(p):
            return cross_ref[k, pl.ds(p, 8, PLANES), :]

        source = {}
        for j in range(max(first, 0), min(last, HALF - 1) + 1):
            beside = crossed(2 * j + 1)
            if j > 0:
                beside += crossed(2 * j - 1)
            source[j] = 0.125 * crossed(2 * j) + 0.0625 * beside
        if h == 0:
            source[-2] = got(4, at)
            source[-1] = got(5, at) + 0.0625 * ours
            source[0] += got(6, at) + (0.125 * theirs + 0.0625 * ours)
        else:
            source[HALF - 1] += 0.0625 * theirs
            after = sent(6, at) + got(4, at) + (0.0625 * theirs + 0.125 * ours)
            source[HALF] = jnp.where(inside, after, 0.0)
            source[HALF + 1] = got(5, at)
            source[HALF + 2] = got(6, at)

        scaled = {j: source[j] * inverse[j] for j in source}
        update = {j: x * (1.0 / CENTER) for j, x in scaled.items()}
        approx = update
        ratio_old = 1.0 / sigma
        for sweep in range(1, DEGREE):
            ratio_new = 1.0 / (2.0 * sigma - ratio_old)
            keep, gain = ratio_new * ratio_old, 2.0 * ratio_new / HALF_WIDTH
            inner = range(first + sweep, last - sweep + 1)
            update = {
                j: keep * update[j]
                + gain * (scaled[j] - approx[j] + quotient[j] * near_sum(approx, j))
                for j in inner
            }
            approx = {j: approx[j] + update[j] for j in inner}
            ratio_old = ratio_new

        for i in range(4):
            here, after = approx[4 * h + i], approx[4 * h + i + 1]
            keep_fix(k, i, here)
            mix_vm[k, eight(2 * i), :] = here
            mix_vm[k, eight(2 * i + 1), :] = 0.5 * (here + after)
    left = []
    for k in range(COMPS):
        mixed = [mix_vm[k, pl.ds(s, 8, 8), :] for s in range(BLOCKS)]
        left += [
            jnp.concatenate([mixed[s], mixed[(s + 1) % BLOCKS]], axis=1) for s in range(BLOCKS)
        ]
    fine = split_dot(jnp.concatenate(left, axis=0), q_ref[...])
    stores = []
    for k in range(COMPS):
        for t in range(TILES):
            add = fine[eight(BLOCKS * k + t // 4), tile(t % 4)]
            out_vm[k, h, eight(t), :] = v_ref[k, h, eight(t), :] + add
        store = pltpu.make_async_copy(out_vm.at[k, h], out_hbm.at[k, h], sems.at[k, h])
        store.start()
        stores.append(store)
    return stores


def upper_kernel(
    left_in,
    right_sent,
    inner_got,
    cross_ref,
    v_ref,
    cv_ref,
    w_ref,
    q_ref,
    left_ref,
    out_hbm,
    fix_ref,
    mix_vm,
    out_vm,
    sems,
):
    del left_in, left_ref

    @pl.when(lax.axis_index("sub") == 0)
    def _():
        def keep_fix(k, i, plane):
            fix_ref[k, eight(i), :] = plane

        stores = finish_half(
            1,
            lambda slab, lanes: right_sent[slab, :, lanes],
            lambda slab, lanes: inner_got[slab, :, lanes],
            cross_ref,
            v_ref,
            cv_ref,
            w_ref,
            q_ref,
            mix_vm,
            out_vm,
            out_hbm,
            sems,
            keep_fix,
        )
        for store in stores:
            store.wait()


def lower_kernel(
    out_in,
    upper_fix,
    left_sent,
    right_got,
    cross_ref,
    v_ref,
    cv_ref,
    w_ref,
    q_ref,
    out_hbm,
    fix_hbm,
    mix_vm,
    out_vm,
    sems,
    fix_vm,
    fix_sem,
):
    del out_in

    @pl.when(lax.axis_index("sub") == 0)
    def _():
        def keep_fix(k, i, plane):
            fix_vm[k, pl.ds(i, 8, 8), :] = plane

        for k in range(COMPS):
            for i in range(4):
                fix_vm[k, pl.ds(4 + i, 8, 8), :] = upper_fix[k, eight(i), :]
        stores = finish_half(
            0,
            lambda slab, lanes: left_sent[slab, :, lanes],
            lambda slab, lanes: right_got[slab, :, lanes],
            cross_ref,
            v_ref,
            cv_ref,
            w_ref,
            q_ref,
            mix_vm,
            out_vm,
            out_hbm,
            sems,
            keep_fix,
        )
        fix_copy = pltpu.make_async_copy(fix_vm, fix_hbm, fix_sem)
        fix_copy.start()
        for store in stores:
            store.wait()
        fix_copy.wait()


def finish_kernel(
    out_in,
    fix_in,
    left_sent,
    right_sent,
    right_got,
    inner_got,
    outer_got,
    cross_ref,
    v_ref,
    cv_ref,
    w_ref,
    q_ref,
    out_hbm,
    fix_hbm,
    mix_vm,
    out_vm,
    sems,
    fix_vm,
    fix_sem,
):
    del out_in, fix_in
    at = lax.axis_index("sub")
    inner = at < lax.axis_size("sub") - 2

    def left_got(slab, lanes):
        return jnp.where(inner, inner_got[slab, :, lanes], outer_got[slab, :, lanes])

    def half(which, sent, got):
        def keep_fix(k, i, plane):
            fix_vm[k, pl.ds(4 * which + i, 8, 8), :] = plane

        refs = (cross_ref, v_ref, cv_ref, w_ref, q_ref, mix_vm, out_vm, out_hbm, sems, keep_fix)
        return finish_half(which, lambda slab, lanes: sent[slab, :, lanes], got, *refs)

    @pl.when(at != 0)
    def _():
        stores = half(0, left_sent, lambda slab, lanes: right_got[slab, :, lanes])
        stores += half(1, right_sent, left_got)
        fix_copy = pltpu.make_async_copy(fix_vm, fix_hbm, fix_sem)
        fix_copy.start()
        for store in stores:
            store.wait()
        fix_copy.wait()


VMEM = pl.BlockSpec(memory_space=pltpu.VMEM)
HBM = pl.BlockSpec(memory_space=pltpu.HBM)
ANY = pl.BlockSpec(memory_space=pl.ANY)
PARAMS = pltpu.CompilerParams(vmem_limit_bytes=16 * 2**20)
FINE_TILED = (2, 8 * TILES, LANES)


def fine_tiled(field):
    lead = field.shape[:-2]
    split = field.reshape(lead + (2, 8, TILES, LANES))
    return jnp.swapaxes(split, -3, -2).reshape(lead + FINE_TILED)


def pinned(field):
    return pltpu.with_memory_space_constraint(field, pltpu.HBM)


def shards(velocity, forcing, viscosity, coarse_visc):
    coeffs = jnp.swapaxes(coarse_visc.reshape(HALF, BLOCKS, LANES), 0, 1).reshape(8 * HALF, LANES)
    message = jax.ShapeDtypeStruct((7, 8, WIDE), F32)
    fine = jax.ShapeDtypeStruct((COMPS,) + FINE_TILED, F32)
    coarse = jax.ShapeDtypeStruct((COMPS, 8 * HALF, LANES), F32)
    crosses = jax.ShapeDtypeStruct((COMPS, 8 * PLANES, LANES), F32)
    right_sent, left_sent, cross, *kept = pl.pallas_call(
        local_kernel,
        out_shape=(
            message,
            message,
            crosses,
            fine,
            jax.ShapeDtypeStruct((8 * HALF, LANES), F32),
            jax.ShapeDtypeStruct((WIDE, 2 * LANES), BF16),
            jax.ShapeDtypeStruct((2 * LANES, WIDE), BF16),
        ),
        in_specs=[HBM] * 4,
        out_specs=(VMEM,) * 7,
        scratch_shapes=[
            pltpu.VMEM((COMPS,) + FINE_TILED, F32),
            pltpu.VMEM(FINE_TILED, F32),
            pltpu.VMEM((2, COMPS * BLOCKS * PLANES, WIDE), BF16),
            pltpu.SemaphoreType.DMA((2 + 2 * COMPS,)),
        ],
        compiler_params=PARAMS,
    )(
        pinned(fine_tiled(velocity)),
        pinned(fine_tiled(forcing)),
        pinned(fine_tiled(viscosity)),
        pinned(coeffs),
    )

    axes = ("grp", "sub")
    count, deep = lax.axis_size(axes), lax.axis_size("sub")
    inner = [(i + 1, i) for i in range(count - 1) if i % deep < deep - 2]
    outer = [(i + 1, i) for i in range(count - 1) if i % deep >= deep - 2]
    right_got = lax.ppermute(right_sent, axes, [(i, i + 1) for i in range(count - 1)])
    inner_got = lax.ppermute(left_sent, axes, inner)
    half_scratch = [
        pltpu.VMEM((COMPS, 8 * 8, LANES), F32),
        pltpu.VMEM((COMPS,) + FINE_TILED, F32),
    ]
    left_sent, corrected, upper_fix = pl.pallas_call(
        upper_kernel,
        out_shape=(message, fine, jax.ShapeDtypeStruct((COMPS, 4 * 8, LANES), F32)),
        in_specs=[ANY] + [VMEM] * 7,
        out_specs=(ANY, HBM, VMEM),
        input_output_aliases={0: 0},
        scratch_shapes=half_scratch + [pltpu.SemaphoreType.DMA((COMPS, 2))],
        compiler_params=PARAMS,
    )(left_sent, right_sent, inner_got, cross, *kept)
    outer_got = lax.ppermute(left_sent, axes, outer)
    finish_scratch = half_scratch + [
        pltpu.SemaphoreType.DMA((COMPS, 2)),
        pltpu.VMEM((COMPS, 8 * HALF, LANES), F32),
        pltpu.SemaphoreType.DMA,
    ]
    corrected, fix = pl.pallas_call(
        lower_kernel,
        out_shape=(fine, coarse),
        in_specs=[HBM] + [VMEM] * 8,
        out_specs=(HBM, HBM),
        input_output_aliases={0: 0},
        scratch_shapes=finish_scratch,
        compiler_params=PARAMS,
    )(pinned(corrected), upper_fix, left_sent, right_got, cross, *kept)
    corrected, fix = pl.pallas_call(
        finish_kernel,
        out_shape=(fine, coarse),
        in_specs=[HBM, HBM] + [VMEM] * 10,
        out_specs=(HBM, HBM),
        input_output_aliases={0: 0, 1: 1},
        scratch_shapes=finish_scratch,
        compiler_params=PARAMS,
    )(
        pinned(corrected),
        pinned(fix),
        left_sent,
        right_sent,
        right_got,
        inner_got,
        outer_got,
        cross,
        *kept,
    )
    corrected = corrected.reshape(COMPS, 2, TILES, 8, LANES)
    fix = fix.reshape(COMPS, BLOCKS, HALF, LANES)
    return (
        jnp.swapaxes(corrected, 2, 3).reshape(velocity.shape),
        jnp.swapaxes(fix, 1, 2).reshape(COMPS, HALF, COARSE),
    )


def solution(mesh):
    return jax.shard_map(
        shards,
        mesh=mesh,
        in_specs=(
            P(None, ("grp", "sub"), None),
            P(None, ("grp", "sub"), None),
            P(("grp", "sub"), None),
            P(("grp", "sub"), None),
        ),
        out_specs=(P(None, ("grp", "sub"), None), P(None, ("grp", "sub"), None)),
        check_vma=False,
    )
```
